256 devices in a mesh: span: 16 (over z_hi, y, core), seq: 16 (over z_lo, x).
Axes of the slice: x: 4, y: 4, z: 8 (z_hi: 2, z_lo: 4; z = z_hi * 4 + z_lo), core: 2. Of those that a mesh axis runs over, the one named last changes fastest.
Arguments:
- query_rows: bfloat16 [12288, 4096], P(('span', 'seq')), may hold values from -8 to 8
- key_rows: bfloat16 [12288, 4096], P(('span', 'seq')), may hold values from -8 to 8
- value_rows: bfloat16 [12288, 4096], P(('span', 'seq')), may hold values from -8 to 8
- token_counts: int32 [16], replicated, may hold values from 384 to 768, as said below
Outputs:
- attended: bfloat16 [12288, 4096], P(('span', 'seq'))
The draws below stay inside these ranges and needn't reach their ends.
Inputs may be any that keep to these rules, and one draw needn't show every extreme that they name: token_counts[b] is the number of real tokens of span b; some span is full.
All inputs are finite; a program needn't handle non-finite values.
Results may differ from the reference program's by a relative error of at most 0.0075.
Values may be sent and summed in bfloat16 or wider, within the bound.
A program may use at most 64 MiB of HBM per device.

```python
import jax
import jax.numpy as jnp
from jax import lax

H = 32
HD = 128
SPANS = 16
LEN = 768
TOKENS = 12288


def draw_query_rows(key, part):
    key = jax.random.fold_in(key, 3)
    base = jnp.clip(jax.random.normal(key, (TOKENS, H * HD), jnp.float32), -8.0, 8.0)
    return base.astype(jnp.bfloat16)


def draw_key_rows(key, part):
    key = jax.random.fold_in(key, 5)
    base = jnp.clip(jax.random.normal(key, (TOKENS, H * HD), jnp.float32), -8.0, 8.0)
    return base.astype(jnp.bfloat16)


def draw_token_counts(key, part):
    key = jax.random.fold_in(key, 7)
    counted = jax.random.randint(key, (SPANS,), LEN // 2, LEN + 1)
    full_at = jax.random.randint(jax.random.fold_in(key, 1), (), 0, SPANS)
    return counted.at[full_at].set(LEN).astype(jnp.int32)


def level_of(stream_key, dims, cuts, smallest, top_value):
    level, own = 1.0, jax.random.fold_in(stream_key, 6)
    for position, blocks in cuts:
        draws = jnp.exp(jax.random.uniform(jax.random.fold_in(own, position), (blocks,), jnp.float32, smallest / len(cuts), top_value / len(cuts)))
        level = level * jnp.repeat(draws, dims[position] // blocks).reshape([-1 if axis == position else 1 for axis in range(len(dims))])
    return level


def noise(key, shape, width, most, split=(), kind=jnp.bfloat16):
    gain = level_of(key, shape, split, -0.22, 0.18) if split else 1.0
    result = jax.random.normal(key, shape, jnp.float32) * width * gain
    return jnp.minimum(jnp.maximum(result, -most), most).astype(kind)


def setup_inputs(seed: int = 0) -> dict:
    key_of = jax.random.split(jax.random.key(seed), 5)
    query_rows = draw_query_rows(jax.random.fold_in(key_of[4], 71), 0)
    key_rows = draw_key_rows(jax.random.fold_in(key_of[4], 71), 0)
    value_rows = noise(key_of[2], (TOKENS, H * HD), 1.0, 8.0, ((0, 256),))
    token_counts = draw_token_counts(jax.random.fold_in(key_of[4], 71), 0)
    return dict(query_rows=query_rows, key_rows=key_rows, value_rows=value_rows, token_counts=token_counts)


def reference(query_rows, key_rows, value_rows, token_counts):
    scaling = HD ** -0.5
    query_grid = query_rows.reshape(TOKENS, H, HD)
    key_grid = key_rows.reshape(TOKENS, H, HD)
    value_grid = value_rows.reshape(TOKENS, H, HD)
    results = []
    for span_id in range(SPANS):
        visible_len = (span_id + 1) * LEN
        query_part = jnp.transpose(query_grid[span_id * LEN:(span_id + 1) * LEN], (1, 0, 2))
        key_part = jnp.transpose(key_grid[:visible_len], (1, 0, 2))
        value_part = jnp.transpose(value_grid[:visible_len], (1, 0, 2))
        positions = jnp.arange(visible_len, dtype=jnp.int32)
        owner = positions // LEN
        key_valid = (positions - owner * LEN) < token_counts[owner]

        def one_head(operands):
            query_head, key_head, value_head = operands
            scores = jnp.dot(query_head, key_head.T, preferred_element_type=jnp.float32) * scaling
            scores = jnp.where(key_valid[None, :], scores, -1e30)
            row_max = jnp.max(scores, axis=1, keepdims=True)
            weights = jnp.where(key_valid[None, :], jnp.exp(scores - row_max), 0.0).astype(jnp.bfloat16)
            numerator = jnp.dot(weights, value_head, preferred_element_type=jnp.float32)
            denominator = jnp.sum(weights.astype(jnp.float32), axis=1)
            return (numerator / denominator[:, None]).astype(jnp.bfloat16)

        heads_out = lax.map(one_head, (query_part, key_part, value_part))
        results.append(jnp.transpose(heads_out, (1, 0, 2)).reshape(LEN, H * HD))
    return jnp.concatenate(results, axis=0)
```

```python
import functools
import math

import jax
import jax.numpy as jnp
from jax import lax
from jax.experimental import pallas as pl
from jax.experimental.pallas import tpu as pltpu
from jax.sharding import PartitionSpec as P

MESH = pl.DeviceIdType.MESH
HD = 128
SPANS = 16
LEN = 768
ROWS = 48
PART = 192
PEERS = 32
NEG = -1e30
LOG2_SCALE = HD ** -0.5 * math.log2(math.e)
VMEM_LIMIT = 56 * 1024 * 1024


class Place:
    def __init__(self):
        self.span = lax.axis_index("span")
        self.seq = lax.axis_index("seq")
        self.core = self.span % 2
        self.y = (self.span // 2) % 4
        self.z = (self.span // 8) * 4 + self.seq // 4
        self.x = self.seq % 4

    def span_of(self, z_hi, y, core):
        return (z_hi * 4 + y) * 2 + core

    def plane(self, t):
        return (self.z + ((t + 1) // 2) * (2 * (t % 2) - 1) + 8) % 8

    def peers(self):
        places = {}
        xs = [self.x] + [(self.x + dx) % 4 for dx in (1, 2, 3)]
        for t in range(8):
            dz = ((t + 1) // 2) * (2 * (t % 2) - 1)
            z = (self.z + dz + 8) % 8
            z_hi, z_lo = z // 4, z % 4
            span = self.span_of(z_hi, self.y, self.core)
            for dx in range(4):
                seq = z_lo * 4 + xs[dx]
                places[t, dx] = ((span, seq), z_hi * 16 + seq)
        return places

    def group(self, g):
        z_hi, z_lo = self.z // 4, self.z % 4
        inner = ((z_lo + 1) // 2) % 2
        other = jnp.where(g == 0, 0, jnp.where(g == 1, 1 - inner, jnp.where(g == 2, inner, 1)))
        moved = jnp.where((g == 1) | (g == 2), 1, 0)
        return (z_hi + other) % 2, (z_lo // 2 + moved) % 2

    def up(self):
        return (self.span_of(self.z // 4, (self.y + 1) % 4, self.core), self.seq)

    def down(self):
        return (self.span_of(self.z // 4, (self.y + 3) % 4, self.core), self.seq)

    def sibling(self):
        return (self.span_of(self.z // 4, self.y, 1 - self.core), self.seq)


def greet(devices):
    barrier = pltpu.get_barrier_semaphore()
    for device in devices:
        pl.semaphore_signal(barrier, inc=1, device_id=device, device_id_type=MESH)
    pl.semaphore_wait(barrier, len(devices))


def remote(src, dst, send_sem, recv_sem, device):
    return pltpu.make_async_remote_copy(
        src_ref=src, dst_ref=dst, send_sem=send_sem, recv_sem=recv_sem,
        device_id=device, device_id_type=MESH)


def arrived(ref, sem):
    pltpu.make_async_copy(ref, ref, sem).wait()


TILE = 256
HALF = LEN // 2


def attend_item(q_index, pair, half, keep_second, counts_ref, q2_ref, kv_ref, m_ref, acc_ref):
    rows = pl.ds(pl.multiple_of(half * HALF, 16), HALF)
    first, second = 2 * pair, 2 * pair + 1
    k = jnp.concatenate([kv_ref[0, first, rows], kv_ref[0, second, rows]], axis=0)
    k2 = jnp.concatenate([k, k], axis=1)
    v = jnp.concatenate([kv_ref[1, first, rows], kv_ref[1, second, rows]], axis=0)
    v2 = jnp.concatenate([v, jnp.ones_like(v)], axis=1)
    lane = lax.broadcasted_iota(jnp.int32, (1, HALF), 1) + half * HALF
    bias = jnp.concatenate([
        jnp.where(lane < counts_ref[first], 0.0, NEG),
        jnp.where(lane < counts_ref[second] * keep_second, 0.0, NEG)], axis=1)
    tiles = LEN // TILE
    scores, probs = [None] * tiles, [None] * tiles

    def at(i):
        return pl.ds(i * TILE, TILE)

    def score(i):
        scores[i] = lax.dot_general(
            q2_ref[q_index, at(i)], k2, (((1,), (1,)), ((), ())), preferred_element_type=jnp.float32)

    def soften(i):
        s = scores[i] + bias
        m_old = m_ref[q_index, at(i)]
        m_new = jnp.maximum(m_old, jnp.max(s, axis=1, keepdims=True))
        wide = jnp.concatenate([m_new] * (LEN // HD), axis=1)
        probs[i] = jnp.exp2(s - wide).astype(jnp.bfloat16)
        m_ref[q_index, at(i)] = m_new
        shrink = jnp.exp2(m_old - m_new)
        acc_ref[q_index, at(i)] = acc_ref[q_index, at(i)] * jnp.concatenate([shrink, shrink], axis=1)

    def gain(i):
        acc_ref[q_index, at(i)] += jnp.dot(probs[i], v2, preferred_element_type=jnp.float32)

    for i in range(tiles + 2):
        if i < tiles:
            score(i)
        if 1 <= i < tiles + 1:
            soften(i - 1)
        if 2 <= i:
            gain(i - 2)


def prepare(z_hi, q_ref, q2_ref, m_ref, acc_ref):
    q = q_ref[z_hi].astype(jnp.float32) * LOG2_SCALE
    high = q.astype(jnp.bfloat16)
    low = (q - high.astype(jnp.float32)).astype(jnp.bfloat16)
    q2_ref[z_hi] = jnp.concatenate([high, low], axis=1)
    m_ref[z_hi] = jnp.full((LEN, HD), NEG, jnp.float32)
    acc_ref[z_hi] = jnp.zeros((LEN, 2 * HD), jnp.float32)


MIRROR = (0, 2, 1, 4, 3, 6, 5, 7)


def messages(*planes):
    return [(t, dx) for dx in range(4) for t in planes if (t, dx) != (0, 0)]


def kernel(counts_ref, q_ref, k_ref, v_ref, out_ref, stage_q, stage_kv, qall, kvall, q2_ref, m_ref, acc_ref, o_ref,
           stage_sem, a2a_send, a2a_recv, q_recv, y_send, up_recv, down_recv, far_recv, sib_recv, o_send, o_recv):
    me = Place()
    up, down, sibling = me.up(), me.down(), me.sibling()
    peers = me.peers()
    own_head = peers[0, 0][1]
    staged = [
        pltpu.make_async_copy(k_ref, stage_kv.at[0], stage_sem.at[0]),
        pltpu.make_async_copy(v_ref, stage_kv.at[1], stage_sem.at[1]),
        pltpu.make_async_copy(q_ref, stage_q, stage_sem.at[2]),
    ]
    for copy in staged:
        copy.start()
    order = messages(0) + messages(1, 2) + messages(3, 4) + messages(5, 6) + messages(7)
    greet([peers[at][0] for at in order] + [up, down, sibling])

    def cols(head):
        return pl.ds(pl.multiple_of(head * HD, HD), HD)

    rows = pl.ds(pl.multiple_of(me.seq * ROWS, 16), ROWS)
    kv_rows = kvall.at[:, me.span, rows]
    q_rows = qall.at[me.z // 4, rows]

    def send_kv(places):
        for t, dx in places:
            device, head = peers[t, dx]
            remote(stage_kv.at[:, :, cols(head)], kv_rows, a2a_send.at[0], a2a_recv.at[MIRROR[t]], device).start()

    def send_q(places):
        for t, dx in places:
            device, head = peers[t, dx]
            remote(stage_q.at[:, cols(head)], q_rows, a2a_send.at[1], q_recv, device).start()

    y_up, y_down, y_far = (me.y + 1) % 4, (me.y + 3) % 4, (me.y + 2) % 4

    def block(t, y, core):
        z = me.plane(t)
        part = pl.ds(pl.multiple_of((z % 4) * PART, 16), PART)
        return me.span_of(z // 4, y, core), part

    def own_part(t):
        span, part = block(t, me.y, me.core)
        ref = kvall.at[:, span, part]
        arrived(ref, a2a_recv.at[t])
        remote(ref, ref, y_send.at[0], up_recv.at[t], up).start()
        remote(ref, ref, y_send.at[1], down_recv.at[t], down).start()
        remote(ref, ref, y_send.at[4], sib_recv.at[t], sibling).start()

    def near_part(t):
        span, part = block(t, y_down, me.core)
        ref = kvall.at[:, span, part]
        arrived(ref, up_recv.at[t])
        half = kvall.at[0, span, part]
        remote(half, half, y_send.at[2], far_recv.at[t], up).start()
        remote(ref, ref, y_send.at[4], sib_recv.at[8 + t], sibling).start()
        span, part = block(t, y_up, me.core)
        ref = kvall.at[:, span, part]
        arrived(ref, down_recv.at[t])
        half = kvall.at[1, span, part]
        remote(half, half, y_send.at[3], far_recv.at[t], down).start()
        remote(ref, ref, y_send.at[4], sib_recv.at[16 + t], sibling).start()

    def far_part(t):
        span, part = block(t, y_far, me.core)
        ref = kvall.at[:, span, part]
        arrived(ref, far_recv.at[t])
        remote(ref, ref, y_send.at[4], sib_recv.at[24 + t], sibling).start()

    def from_sibling(j, y, t):
        span, part = block(t, y, 1 - me.core)
        arrived(kvall.at[:, span, part], sib_recv.at[8 * j + t])

    def each(first, last, part):
        lax.fori_loop(first, last, lambda t, _: (part(t), 0)[1], 0)

    to = cols(own_head)

    def finish(h):
        o_ref[h] = (acc_ref[h, :, :HD] / acc_ref[h, :, HD:]).astype(jnp.bfloat16)

        @pl.when(me.z // 4 == h)
        def _():
            piece = o_ref.at[h, rows]
            pltpu.make_async_copy(piece, out_ref.at[:, to], o_recv).start()

        for place in order:
            device, head = peers[place]

            @pl.when(head // 16 == h)
            def _():
                piece = o_ref.at[h, pl.ds(pl.multiple_of((head % 16) * ROWS, 16), ROWS)]
                remote(piece, out_ref.at[:, to], o_send, o_recv, device).start()

    for copy in staged[:2]:
        copy.wait()
    pltpu.make_async_copy(stage_kv.at[:, :, to], kv_rows, a2a_recv.at[0]).start()
    send_kv(messages(0))
    send_kv(messages(1, 2))
    staged[2].wait()
    pltpu.make_async_copy(stage_q.at[:, to], q_rows, q_recv).start()
    send_q(order[:15])
    own_part(0)
    send_q(order[15:])
    own_part(1)
    own_part(2)
    send_kv(messages(3, 4))
    near_part(0)
    send_kv(messages(5, 6))
    send_kv(messages(7))
    near_part(1)
    near_part(2)
    each(0, 3, far_part)
    arrived(qall, q_recv)
    each(0, 2, lambda h: prepare(h, qall, q2_ref, m_ref, acc_ref))
    each(0, 1, functools.partial(from_sibling, 0, me.y))
    each(0, 1, functools.partial(from_sibling, 1, y_down))
    each(0, 1, functools.partial(from_sibling, 2, y_up))
    each(0, 1, functools.partial(from_sibling, 3, y_far))

    def step(i, _):
        g, j = i // 4, i % 4
        near, far = 2 * g + 1, jnp.minimum(2 * g + 3, 8)
        more, most = 2 * g + 3, jnp.where(g < 3, jnp.minimum(2 * g + 5, 8), 2 * g + 3)

        @pl.when(j == 0)
        def _():
            each(near, far, functools.partial(from_sibling, 0, me.y))

        @pl.when(j == 1)
        def _():
            each(more, jnp.minimum(more + 1, most), own_part)
            each(near, far, functools.partial(from_sibling, 1, y_down))

        @pl.when(j == 2)
        def _():
            each(more + 1, most, own_part)

            @pl.when(g >= 1)
            def _():
                each(near, far, far_part)

            each(near, far, functools.partial(from_sibling, 2, y_up))

        @pl.when(j == 3)
        def _():
            each(more, most, near_part)
            each(near, far, functools.partial(from_sibling, 3, y_far))

        y = (me.y + jnp.where(j == 0, 0, jnp.where(j == 1, 3, jnp.where(j == 2, 1, 2)))) % 4
        z_hi, half = me.group(g)
        pair = z_hi * 4 + y

        def item(q_index, _):
            own = q_index * 4 + me.y

            @pl.when(pair <= own)
            def _():
                keep = jnp.where((pair < own) | (me.core == 1), 1, 0)
                attend_item(q_index, pair, half, keep, counts_ref, q2_ref, kvall, m_ref, acc_ref)

            return 0

        lax.fori_loop(0, 2, item, 0)

        @pl.when((i == 11) & (me.z < 4))
        def _():
            finish(0)

        return 0

    lax.fori_loop(0, 16, step, 0)

    @pl.when(me.z >= 4)
    def _():
        finish(0)

    finish(1)

    sent = pl.ds(0, (PEERS - 1) * HD)
    arrived(stage_kv.at[:, :, sent], a2a_send.at[0])
    arrived(stage_q.at[:, sent], a2a_send.at[1])
    for j, ref in enumerate((kvall.at[:, 0:2], kvall.at[:, 0:2], kvall.at[0, 0:2], kvall.at[0, 0:2], kvall.at[:, 0:8])):
        arrived(ref, y_send.at[j])
    arrived(out_ref, o_recv)
    arrived(out_ref.at[:, sent], o_send)


def on_device(query_rows, key_rows, value_rows, token_counts):
    any_spec = pl.BlockSpec(memory_space=pl.ANY)
    dma = pltpu.SemaphoreType.DMA
    return pl.pallas_call(
        kernel,
        out_shape=jax.ShapeDtypeStruct((ROWS, PEERS * HD), jnp.bfloat16),
        in_specs=[pl.BlockSpec(memory_space=pltpu.SMEM), any_spec, any_spec, any_spec],
        out_specs=any_spec,
        scratch_shapes=[
            pltpu.VMEM((ROWS, PEERS * HD), jnp.bfloat16), pltpu.VMEM((2, ROWS, PEERS * HD), jnp.bfloat16),
            pltpu.VMEM((2, LEN, HD), jnp.bfloat16), pltpu.VMEM((2, SPANS, LEN, HD), jnp.bfloat16),
            pltpu.VMEM((2, LEN, 2 * HD), jnp.bfloat16), pltpu.VMEM((2, LEN, HD), jnp.float32),
            pltpu.VMEM((2, LEN, 2 * HD), jnp.float32), pltpu.VMEM((2, LEN, HD), jnp.bfloat16),
            dma((3,)), dma((2,)), dma((8,)), dma, dma((5,)), dma((8,)), dma((8,)), dma((8,)), dma((32,)), dma, dma],
        compiler_params=pltpu.CompilerParams(collective_id=0, has_side_effects=True, vmem_limit_bytes=VMEM_LIMIT),
        name="span_attention",
    )(token_counts, query_rows, key_rows, value_rows)


def solution(mesh):
    rows = P(("span", "seq"), None)
    return jax.shard_map(
        on_device, mesh=mesh, in_specs=(rows, rows, rows, P()), out_specs=rows, check_vma=False)
```

```python
import functools
import math

import jax
import jax.numpy as jnp
from jax import lax
from jax.experimental import pallas as pl
from jax.experimental.pallas import tpu as pltpu
from jax.sharding import PartitionSpec as P

MESH = pl.DeviceIdType.MESH
HD = 128
SPANS = 16
LEN = 768
ROWS = 48
PART = 192
PEERS = 32
NEG = -1e30
LOG2_SCALE = HD ** -0.5 * math.log2(math.e)
VMEM_LIMIT = 56 * 1024 * 1024


class Place:
    def __init__(self):
        self.span = lax.axis_index("span")
        self.seq = lax.axis_index("seq")
        self.core = self.span % 2
        self.y = (self.span // 2) % 4
        self.z = (self.span // 8) * 4 + self.seq // 4
        self.x = self.seq % 4

    def span_of(self, z_hi, y, core):
        return (z_hi * 4 + y) * 2 + core

    def plane(self, t):
        return (self.z + ((t + 1) // 2) * (2 * (t % 2) - 1) + 8) % 8

    def peers(self):
        places = {}
        xs = [self.x] + [(self.x + dx) % 4 for dx in (1, 2, 3)]
        for t in range(8):
            dz = ((t + 1) // 2) * (2 * (t % 2) - 1)
            z = (self.z + dz + 8) % 8
            z_hi, z_lo = z // 4, z % 4
            span = self.span_of(z_hi, self.y, self.core)
            for dx in range(4):
                seq = z_lo * 4 + xs[dx]
                places[t, dx] = ((span, seq), z_hi * 16 + seq)
        return places

    def group(self, g):
        z_hi, z_lo = self.z // 4, self.z % 4
        inner = ((z_lo + 1) // 2) % 2
        other = jnp.where(g == 0, 0, jnp.where(g == 1, 1 - inner, jnp.where(g == 2, inner, 1)))
        moved = jnp.where((g == 1) | (g == 2), 1, 0)
        return (z_hi + other) % 2, (z_lo // 2 + moved) % 2

    def up(self):
        return (self.span_of(self.z // 4, (self.y + 1) % 4, self.core), self.seq)

    def down(self):
        return (self.span_of(self.z // 4, (self.y + 3) % 4, self.core), self.seq)

    def sibling(self):
        return (self.span_of(self.z // 4, self.y, 1 - self.core), self.seq)


def greet(devices):
    barrier = pltpu.get_barrier_semaphore()
    for device in devices:
        pl.semaphore_signal(barrier, inc=1, device_id=device, device_id_type=MESH)
    pl.semaphore_wait(barrier, len(devices))


def remote(src, dst, send_sem, recv_sem, device):
    return pltpu.make_async_remote_copy(
        src_ref=src, dst_ref=dst, send_sem=send_sem, recv_sem=recv_sem,
        device_id=device, device_id_type=MESH)


def arrived(ref, sem):
    pltpu.make_async_copy(ref, ref, sem).wait()


TILE = 256
HALF = LEN // 2


def attend_item(q_index, spans, limits, half, q2_ref, kv_ref, m_ref, acc_ref):
    rows = pl.ds(pl.multiple_of(half * HALF, 16), HALF)
    k = jnp.concatenate([kv_ref[0, span, rows] for span in spans], axis=0)
    k2 = jnp.concatenate([k, k], axis=1)
    v = jnp.concatenate([kv_ref[1, span, rows] for span in spans], axis=0)
    v2 = jnp.concatenate([v, jnp.ones_like(v)], axis=1)
    lane = lax.broadcasted_iota(jnp.int32, (1, HALF), 1) + half * HALF
    bias = jnp.concatenate([jnp.where(lane < limit, 0.0, NEG) for limit in limits], axis=1)
    tiles = LEN // TILE
    scores, probs = [None] * tiles, [None] * tiles

    def at(i):
        return pl.ds(i * TILE, TILE)

    def score(i):
        scores[i] = lax.dot_general(
            q2_ref[q_index, at(i)], k2, (((1,), (1,)), ((), ())), preferred_element_type=jnp.float32)

    def soften(i):
        s = scores[i] + bias
        m_old = m_ref[q_index, at(i)]
        m_new = jnp.maximum(m_old, jnp.max(s, axis=1, keepdims=True))
        wide = jnp.concatenate([m_new] * (LEN // HD), axis=1)
        probs[i] = jnp.exp2(s - wide).astype(jnp.bfloat16)
        m_ref[q_index, at(i)] = m_new
        shrink = jnp.exp2(m_old - m_new)
        acc_ref[q_index, at(i)] = acc_ref[q_index, at(i)] * jnp.concatenate([shrink, shrink], axis=1)

    def gain(i):
        acc_ref[q_index, at(i)] += jnp.dot(probs[i], v2, preferred_element_type=jnp.float32)

    for i in range(tiles + 2):
        if i < tiles:
            score(i)
        if 1 <= i < tiles + 1:
            soften(i - 1)
        if 2 <= i:
            gain(i - 2)


def prepare(i, q_ref, q2_ref, m_ref, acc_ref):
    q = q_ref[i].astype(jnp.float32) * LOG2_SCALE
    high = q.astype(jnp.bfloat16)
    low = (q - high.astype(jnp.float32)).astype(jnp.bfloat16)
    q2_ref[i] = jnp.concatenate([high, low], axis=1)
    m_ref[i] = jnp.full((LEN, HD), NEG, jnp.float32)
    acc_ref[i] = jnp.zeros((LEN, 2 * HD), jnp.float32)


MIRROR = (0, 2, 1, 4, 3, 6, 5, 7)


def messages(*planes):
    return [(t, dx) for dx in range(4) for t in planes if (t, dx) != (0, 0)]


def kernel(counts_ref, q_ref, k_ref, v_ref, out_ref, stage_q, stage_kv, qall, kvall, q2_ref, m_ref, acc_ref, o_ref,
           part_out, part_in, stage_sem, a2a_send, a2a_recv, q_recv, y_send, up_recv, down_recv, far_recv, sib_send,
           sib_recv, part_recv, o_send, o_recv):
    me = Place()
    up, down, sibling = me.up(), me.down(), me.sibling()
    peers = me.peers()
    own_head = peers[0, 0][1]
    z_half = me.z // 4
    staged = [
        pltpu.make_async_copy(k_ref, stage_kv.at[0], stage_sem.at[0]),
        pltpu.make_async_copy(v_ref, stage_kv.at[1], stage_sem.at[1]),
        pltpu.make_async_copy(q_ref, stage_q, stage_sem.at[2]),
    ]
    for copy in staged:
        copy.start()
    order = messages(0) + messages(1, 2) + messages(3, 4) + messages(5, 6) + messages(7)
    greet([peers[at][0] for at in order] + [up, down, sibling])

    def cols(head):
        return pl.ds(pl.multiple_of(head * HD, HD), HD)

    rows = pl.ds(pl.multiple_of(me.seq * ROWS, 16), ROWS)
    kv_rows = kvall.at[:, me.span // 2, rows]
    q_rows = qall.at[2 + z_half, rows]

    def send_kv(places):
        for t, dx in places:
            device, head = peers[t, dx]
            remote(stage_kv.at[:, :, cols(head)], kv_rows, a2a_send.at[0], a2a_recv.at[MIRROR[t]], device).start()

    def send_q(places):
        for t, dx in places:
            device, head = peers[t, dx]
            remote(stage_q.at[:, cols(head)], q_rows, a2a_send.at[1], q_recv, device).start()

    y_up, y_down, y_far = (me.y + 1) % 4, (me.y + 3) % 4, (me.y + 2) % 4

    def block(t, y):
        z = me.plane(t)
        part = pl.ds(pl.multiple_of((z % 4) * PART, 16), PART)
        return (z // 4) * 4 + y, part

    def own_part(t):
        span, part = block(t, me.y)
        ref = kvall.at[:, span, part]
        arrived(ref, a2a_recv.at[t])
        remote(ref, ref, y_send.at[0], up_recv.at[t], up).start()
        remote(ref, ref, y_send.at[1], down_recv.at[t], down).start()

    def near_part(t):
        span, part = block(t, y_down)
        arrived(kvall.at[:, span, part], up_recv.at[t])
        half = kvall.at[0, span, part]
        remote(half, half, y_send.at[2], far_recv.at[t], up).start()
        span, part = block(t, y_up)
        arrived(kvall.at[:, span, part], down_recv.at[t])
        half = kvall.at[1, span, part]
        remote(half, half, y_send.at[3], far_recv.at[t], down).start()

    def far_part(t):
        span, part = block(t, y_far)
        arrived(kvall.at[:, span, part], far_recv.at[t])

    def each(first, last, part):
        lax.fori_loop(first, last, lambda t, _: (part(t), 0)[1], 0)

    to = cols(own_head)

    def give(h):
        lane = lax.broadcasted_iota(jnp.int32, (LEN, HD), 1)
        part_out[h, 0] = acc_ref[h, :, :HD]
        part_out[h, 1] = jnp.where(lane < HD // 2, m_ref[h], acc_ref[h, :, HD:])
        remote(part_out.at[h], part_in.at[h], sib_send.at[1 + h], part_recv.at[h], sibling).start()

    def finish(h):
        arrived(part_in.at[h], part_recv.at[h])
        mine, theirs = m_ref[2 + h], part_in[h, 1, :, :1]
        top = jnp.maximum(mine, theirs)
        keep, add = jnp.exp2(mine - top), jnp.exp2(theirs - top)
        total = acc_ref[2 + h, :, HD:] * keep + part_in[h, 1, :, HD // 2:HD // 2 + 1] * add
        o_ref[h] = ((acc_ref[2 + h, :, :HD] * keep + part_in[h, 0] * add) / total).astype(jnp.bfloat16)

        @pl.when(z_half == h)
        def _():
            pltpu.make_async_copy(o_ref.at[h, rows], out_ref.at[:, to], o_recv).start()

        for t in range(8):
            @pl.when(peers[t, 0][1] // 16 == h)
            def _():
                for dx in range(1 if t == 0 else 0, 4):
                    device, head = peers[t, dx]
                    piece = o_ref.at[h, pl.ds(pl.multiple_of((head % 16) * ROWS, 16), ROWS)]
                    remote(piece, out_ref.at[:, to], o_send, o_recv, device).start()

    for copy in staged[:2]:
        copy.wait()
    pltpu.make_async_copy(stage_kv.at[:, :, to], kv_rows, a2a_recv.at[0]).start()
    send_kv(messages(0))
    send_kv(messages(1, 2))
    staged[2].wait()
    pltpu.make_async_copy(stage_q.at[:, to], q_rows, q_recv).start()
    send_q(order[:15])
    own_part(0)
    send_q(order[15:])
    own_part(1)
    own_part(2)
    send_kv(messages(3, 4))
    near_part(0)
    send_kv(messages(5, 6))
    send_kv(messages(7))
    near_part(1)
    near_part(2)
    arrived(qall.at[2:4], q_recv)
    to_sibling = remote(qall.at[2:4], qall.at[0:2], sib_send.at[0], sib_recv, sibling)
    to_sibling.start()
    each(2, 4, lambda i: prepare(i, qall, q2_ref, m_ref, acc_ref))
    each(0, 3, far_part)
    to_sibling.wait_recv()
    each(0, 2, lambda i: prepare(i, qall, q2_ref, m_ref, acc_ref))

    def step(i, _):
        g, second = i // 2, i % 2
        near, far = 2 * g + 1, jnp.minimum(2 * g + 3, 8)
        more, most = 2 * g + 3, jnp.where(g < 3, jnp.minimum(2 * g + 5, 8), 2 * g + 3)

        @pl.when((g >= 1) & (second == 0))
        def _():
            each(near, far, near_part)

        @pl.when(second == 1)
        def _():
            @pl.when(g >= 1)
            def _():
                each(near, far, far_part)

            each(more + 1, most, own_part)

        @pl.when((i == 7) & (me.z < 4))
        def _():
            finish(0)

        z_hi, half = me.group(g)
        ys = (jnp.where(second == 0, y_down, me.y), jnp.where(second == 0, y_up, y_far))

        def item(q_index, _):
            @pl.when((second == 0) & (q_index == 2))
            def _():
                each(more, jnp.minimum(more + 1, most), own_part)

            h = q_index % 2
            core = jnp.where(q_index < 2, 1 - me.core, me.core)
            own = 2 * (h * 4 + me.y) + core
            spans = [z_hi * 4 + y for y in ys]
            seen = [2 * span + me.core <= own for span in spans]
            limits = [jnp.where(see, counts_ref[2 * span + me.core], 0) for see, span in zip(seen, spans)]

            @pl.when(seen[0] | seen[1])
            def _():
                attend_item(q_index, spans, limits, half, q2_ref, kvall, m_ref, acc_ref)

            @pl.when((q_index == 0) & (i == jnp.where(me.z < 4, 5, 7)))
            def _():
                give(0)

            return 0

        lax.fori_loop(0, 2, item, 0)

        @pl.when(i == 7)
        def _():
            give(1)

        lax.fori_loop(2, 4, item, 0)
        return 0

    lax.fori_loop(0, 8, step, 0)

    @pl.when(me.z >= 4)
    def _():
        finish(0)

    finish(1)

    sent = pl.ds(0, (PEERS - 1) * HD)
    arrived(stage_kv.at[:, :, sent], a2a_send.at[0])
    arrived(stage_q.at[:, sent], a2a_send.at[1])
    for j, ref in enumerate((kvall.at[:, 0:2], kvall.at[:, 0:2], kvall.at[0, 0:2], kvall.at[0, 0:2])):
        arrived(ref, y_send.at[j])
    to_sibling.wait_send()
    for h in range(2):
        arrived(part_out.at[h], sib_send.at[1 + h])
    arrived(out_ref, o_recv)
    arrived(out_ref.at[:, sent], o_send)


def on_device(query_rows, key_rows, value_rows, token_counts):
    any_spec = pl.BlockSpec(memory_space=pl.ANY)
    dma = pltpu.SemaphoreType.DMA
    return pl.pallas_call(
        kernel,
        out_shape=jax.ShapeDtypeStruct((ROWS, PEERS * HD), jnp.bfloat16),
        in_specs=[pl.BlockSpec(memory_space=pltpu.SMEM), any_spec, any_spec, any_spec],
        out_specs=any_spec,
        scratch_shapes=[
            pltpu.VMEM((ROWS, PEERS * HD), jnp.bfloat16), pltpu.VMEM((2, ROWS, PEERS * HD), jnp.bfloat16),
            pltpu.VMEM((4, LEN, HD), jnp.bfloat16), pltpu.VMEM((2, SPANS // 2, LEN, HD), jnp.bfloat16),
            pltpu.VMEM((4, LEN, 2 * HD), jnp.bfloat16), pltpu.VMEM((4, LEN, HD), jnp.float32),
            pltpu.VMEM((4, LEN, 2 * HD), jnp.float32), pltpu.VMEM((2, LEN, HD), jnp.bfloat16),
            pltpu.VMEM((2, 2, LEN, HD), jnp.float32), pltpu.VMEM((2, 2, LEN, HD), jnp.float32),
            dma((3,)), dma((2,)), dma((8,)), dma, dma((4,)), dma((8,)), dma((8,)), dma((8,)), dma((3,)), dma,
            dma((2,)), dma, dma],
        compiler_params=pltpu.CompilerParams(collective_id=0, has_side_effects=True, vmem_limit_bytes=VMEM_LIMIT),
        name="span_attention",
    )(token_counts, query_rows, key_rows, value_rows)


def solution(mesh):
    rows = P(("span", "seq"), None)
    return jax.shard_map(
        on_device, mesh=mesh, in_specs=(rows, rows, rows, P()), out_specs=rows, check_vma=False)
```

```python
import functools
import math

import jax
import jax.numpy as jnp
from jax import lax
from jax.experimental import pallas as pl
from jax.experimental.pallas import tpu as pltpu
from jax.sharding import PartitionSpec as P

MESH = pl.DeviceIdType.MESH
HD = 128
SPANS = 16
LEN = 768
ROWS = 48
PART = 192
PEERS = 32
NEG = -1e30
LOG2_SCALE = HD ** -0.5 * math.log2(math.e)
VMEM_LIMIT = 56 * 1024 * 1024


class Place:
    def __init__(self):
        self.span = lax.axis_index("span")
        self.seq = lax.axis_index("seq")
        self.core = self.span % 2
        self.y = (self.span // 2) % 4
        self.z = (self.span // 8) * 4 + self.seq // 4
        self.x = self.seq % 4

    def span_of(self, z_hi, y, core):
        return (z_hi * 4 + y) * 2 + core

    def plane(self, t):
        return (self.z + ((t + 1) // 2) * (2 * (t % 2) - 1) + 8) % 8

    def turn_of(self, z):
        d = (z - self.z + 8) % 8
        return jnp.where(d > 4, 2 * (8 - d), jnp.maximum(2 * d - 1, 0))

    def peers(self):
        places = {}
        xs = [self.x] + [(self.x + dx) % 4 for dx in (1, 2, 3)]
        for t in range(8):
            dz = ((t + 1) // 2) * (2 * (t % 2) - 1)
            z = (self.z + dz + 8) % 8
            z_hi, z_lo = z // 4, z % 4
            span = self.span_of(z_hi, self.y, self.core)
            for dx in range(4):
                seq = z_lo * 4 + xs[dx]
                places[t, dx] = ((span, seq), z_hi * 16 + seq)
        return places

    def group(self, g):
        z_hi, z_lo = self.z // 4, self.z % 4
        inner = ((z_lo + 1) // 2) % 2
        other = jnp.where(g == 0, 0, jnp.where(g == 1, 1 - inner, jnp.where(g == 2, inner, 1)))
        moved = jnp.where((g == 1) | (g == 2), 1, 0)
        return (z_hi + other) % 2, (z_lo // 2 + moved) % 2

    def up(self):
        return (self.span_of(self.z // 4, (self.y + 1) % 4, self.core), self.seq)

    def down(self):
        return (self.span_of(self.z // 4, (self.y + 3) % 4, self.core), self.seq)

    def sibling(self):
        return (self.span_of(self.z // 4, self.y, 1 - self.core), self.seq)


def greet(devices):
    barrier = pltpu.get_barrier_semaphore()
    for device in devices:
        pl.semaphore_signal(barrier, inc=1, device_id=device, device_id_type=MESH)
    pl.semaphore_wait(barrier, len(devices))


def remote(src, dst, send_sem, recv_sem, device):
    return pltpu.make_async_remote_copy(
        src_ref=src, dst_ref=dst, send_sem=send_sem, recv_sem=recv_sem,
        device_id=device, device_id_type=MESH)


def arrived(ref, sem):
    pltpu.make_async_copy(ref, ref, sem).wait()


TILE = 256
HALF = LEN // 2


def attend_item(q_indices, segments, x, masked, q2_ref, kv_ref, m_ref, acc_ref):
    k = jnp.concatenate([kv_ref[j, t, :, 0].reshape(PART, HD) for j, t, _ in segments], axis=0)
    k2 = jnp.concatenate([k, k], axis=1)
    v = jnp.concatenate([kv_ref[j, t, :, 1].reshape(PART, HD) for j, t, _ in segments], axis=0)
    v2 = jnp.concatenate([v, jnp.ones_like(v)], axis=1)
    if masked:
        lane = lax.broadcasted_iota(jnp.int32, (1, PART), 1)
        turn = sum(jnp.where(lane >= n * ROWS, 1, 0) for n in (1, 2, 3))
        at_x = x + turn
        row = lane + (jnp.where(at_x >= 4, at_x - 4, at_x) - turn) * ROWS
        bias = jnp.concatenate([jnp.where(row < limit, 0.0, NEG) for _, _, limit in segments], axis=1)
    tiles = [(q, pl.ds(i * TILE, TILE)) for q in q_indices for i in range(LEN // TILE)]
    scores, probs, shrinks = {}, {}, {}

    def score(i):
        q, at = tiles[i]
        scores[i] = lax.dot_general(q2_ref[q, at], k2, (((1,), (1,)), ((), ())), preferred_element_type=jnp.float32)

    def soften(i):
        q, at = tiles[i]
        s = scores.pop(i)
        if masked:
            s = s + bias
        m_old = m_ref[q, at]
        m_new = jnp.maximum(m_old, jnp.max(s, axis=1, keepdims=True))
        probs[i] = jnp.exp2(s - jnp.concatenate([m_new] * (LEN // HD), axis=1)).astype(jnp.bfloat16)
        m_ref[q, at] = m_new
        shrinks[i] = jnp.exp2(m_old - m_new)

    def gain(i):
        q, at = tiles[i]
        shrink = shrinks.pop(i)
        acc_ref[q, at] = acc_ref[q, at] * jnp.concatenate([shrink, shrink], axis=1) + jnp.dot(
            probs.pop(i), v2, preferred_element_type=jnp.float32)

    for i in range(len(tiles) + 2):
        if i < len(tiles):
            score(i)
        if 1 <= i < len(tiles) + 1:
            soften(i - 1)
        if 2 <= i:
            gain(i - 2)


def prepare(i, q, q2_ref, m_ref, acc_ref):
    q = q.astype(jnp.float32) * LOG2_SCALE
    high = q.astype(jnp.bfloat16)
    low = (q - high.astype(jnp.float32)).astype(jnp.bfloat16)
    q2_ref[i] = jnp.concatenate([high, low], axis=1)
    m_ref[i] = jnp.full((LEN, HD), NEG, jnp.float32)
    acc_ref[i] = jnp.zeros((LEN, 2 * HD), jnp.float32)


MIRROR = (0, 2, 1, 4, 3, 6, 5, 7)


LEVELS = ((0, 1), (1, 3), (3, 5), (5, 7), (7, 8))


def kernel(counts_ref, q_ref, k_ref, v_ref, out_ref, stage, z_kv, z_q, kv, qall, q2_ref, m_ref, acc_ref, o_ref,
           part_out, part_in, stage_sem, z_send, z_recv, zq_recv, x_send, x_recv, q_recv, y_send, up_recv, down_recv,
           far_recv, sib_send, part_recv, o_send, o_recv):
    me = Place()
    up, down, sibling = me.up(), me.down(), me.sibling()
    peers = me.peers()
    own_head = peers[0, 0][1]
    z_half = me.z // 4
    staged = [pltpu.make_async_copy(ref, stage.at[i], stage_sem.at[i]) for i, ref in enumerate((k_ref, v_ref, q_ref))]
    for copy in staged:
        copy.start()
    across = [(me.span + 1 - 2 * me.core, peers[0, dx][0][1]) for dx in range(4)]
    greet([device for device, _ in list(peers.values())[1:]] + [up, down] + across)

    def cols(head, heads=1):
        return pl.ds(pl.multiple_of(head * HD, HD), heads * HD)

    x_cols = [cols(peers[0, dx][1] - 4 * me.z) for dx in range(4)]

    def send_z_kv(level):
        for t in range(*LEVELS[level]):
            device, head = peers[t, 0]
            there = MIRROR[t]
            remote(stage.at[pl.ds(0, 2), :, cols(head - me.x, 4)], z_kv.at[there], z_send.at[0],
                   z_recv.at[(there + 1) // 2], device).start()

    def send_z_q(level):
        for t in range(*LEVELS[level]):
            device, head = peers[t, 0]
            there = MIRROR[t]
            remote(stage.at[2, :, cols(head - me.x, 4)], z_q.at[there], z_send.at[1],
                   zq_recv.at[0 if there < 5 else 1], device).start()

    def send_x_kv(level):
        t = pl.ds(LEVELS[level][0], LEVELS[level][1] - LEVELS[level][0])
        if level:
            arrived(z_kv.at[t], z_recv.at[level])
        for dx in range(4):
            if level:
                source, place = z_kv.at[t, :, :, x_cols[dx]], kv.at[0, t, (4 - dx) % 4]
            else:
                source, place = stage.at[pl.ds(0, 2), :, cols(peers[0, dx][1])], kv.at[0, 0, (4 - dx) % 4]
            if dx:
                remote(source, place, x_send.at[0], x_recv.at[level], peers[0, dx][0]).start()
            else:
                pltpu.make_async_copy(source, place, x_recv.at[level]).start()

    def send_x_q(part):
        t = (0, pl.ds(1, 4), pl.ds(5, 3))[part]
        if part:
            arrived(z_q.at[t], zq_recv.at[part - 1])
        for dx in range(4):
            source = z_q.at[t, :, x_cols[dx]] if part else stage.at[2, :, cols(peers[0, dx][1])]
            place = qall.at[1, t, (4 - dx) % 4]
            if dx:
                remote(source, place, x_send.at[1], q_recv, peers[0, dx][0]).start()
            else:
                pltpu.make_async_copy(source, place, q_recv).start()
            remote(source, qall.at[0, t, (4 - dx) % 4], x_send.at[2], q_recv, across[dx]).start()

    def own_part(level):
        t = pl.ds(LEVELS[level][0], LEVELS[level][1] - LEVELS[level][0])
        arrived(kv.at[0, t], x_recv.at[level])
        remote(kv.at[0, t], kv.at[1, t], y_send.at[0], up_recv.at[level], up).start()
        remote(kv.at[0, t], kv.at[2, t], y_send.at[1], down_recv.at[level], down).start()

    def near_part(level):
        t = pl.ds(LEVELS[level][0], LEVELS[level][1] - LEVELS[level][0])
        arrived(kv.at[1, t], up_recv.at[level])
        remote(kv.at[1, t, pl.ds(0, 2)], kv.at[3, t, pl.ds(0, 2)], y_send.at[2], far_recv.at[level], up).start()
        arrived(kv.at[2, t], down_recv.at[level])
        remote(kv.at[2, t, pl.ds(2, 2)], kv.at[3, t, pl.ds(2, 2)], y_send.at[3], far_recv.at[level], down).start()

    def far_part(level):
        t = pl.ds(LEVELS[level][0], LEVELS[level][1] - LEVELS[level][0])
        arrived(kv.at[3, t], far_recv.at[level])

    def give(h):
        lane = lax.broadcasted_iota(jnp.int32, (LEN, HD), 1)
        part_out[h, 0] = acc_ref[h, :, :HD]
        part_out[h, 1] = jnp.where(lane < HD // 2, m_ref[h], acc_ref[h, :, HD:])
        remote(part_out.at[h], part_in.at[h], sib_send.at[h], part_recv.at[h], sibling).start()

    to = cols(own_head)

    def finish(h):
        arrived(part_in.at[h], part_recv.at[h])
        mine, theirs = m_ref[2 + h], part_in[h, 1, :, :1]
        top = jnp.maximum(mine, theirs)
        keep, add = jnp.exp2(mine - top), jnp.exp2(theirs - top)
        total = acc_ref[2 + h, :, HD:] * keep + part_in[h, 1, :, HD // 2:HD // 2 + 1] * add
        o_ref[h] = ((acc_ref[2 + h, :, :HD] * keep + part_in[h, 0] * add) / total).astype(jnp.bfloat16)

        for t in range(8):
            @pl.when(peers[t, 0][1] // 16 == h)
            def _():
                first = pl.multiple_of((peers[t, 0][1] % 16) // 4 * PART, 16)
                for s in range(4):
                    piece = o_ref.at[h, pl.ds(first + s * ROWS, ROWS)]
                    if t or s:
                        remote(piece, out_ref.at[:, to], o_send, o_recv, peers[t, s][0]).start()
                    else:
                        pltpu.make_async_copy(piece, out_ref.at[:, to], o_recv).start()

    def prepare_span(k, h):
        q = [qall[k, me.turn_of(4 * h + z_lo)].reshape(PART, HD) for z_lo in range(4)]
        prepare(2 * k + h, jnp.concatenate(q, axis=0), q2_ref, m_ref, acc_ref)

    for copy in staged[:2]:
        copy.wait()
    send_z_kv(1)
    send_x_kv(0)
    staged[2].wait()
    for level in (1, 2, 3, 4):
        send_z_q(level)
    for level in (2, 3, 4):
        send_z_kv(level)
    send_x_q(0)
    own_part(0)
    send_x_kv(1)
    near_part(0)
    own_part(1)
    send_x_q(1)
    near_part(1)
    send_x_q(2)
    far_part(0)
    send_x_kv(2)
    far_part(1)
    arrived(qall, q_recv)
    lax.fori_loop(0, 4, lambda i, _: (prepare_span(i // 2, i % 2), 0)[1], 0)

    before = {1: [(send_x_kv, 3)], 2: [(near_part, 2)], 3: [(far_part, 2), (send_x_kv, 4)], 4: [(near_part, 3)],
              5: [(far_part, 3)], 6: [(near_part, 4)], 7: [(far_part, 4)]}
    amid = {0: [(own_part, 2)], 2: [(own_part, 3)], 4: [(own_part, 4)]}

    def step(i, _):
        g, second = i // 2, i % 2
        for at, events in before.items():
            @pl.when(i == at)
            def _():
                for part, level in events:
                    part(level)

        @pl.when((i == 7) & (me.z < 4))
        def _():
            finish(0)

        z_hi, half = me.group(g)
        plane = z_hi * 4 + half * 2
        turns = (me.turn_of(plane), me.turn_of(plane + 1))
        places = (jnp.where(second == 0, 1, 0), jnp.where(second == 0, 2, 3))
        ys = [(me.y + jnp.where(second == 0, n, f)) % 4 for n, f in ((3, 0), (1, 2))]

        spans = [2 * (z_hi * 4 + y) + me.core for y in ys]
        last = i == 7

        def segments_for(own):
            limits = [jnp.where(span <= own, counts_ref[span], 0) for span in spans]
            return [(j, t, limit - (half * 2 + n) * PART) for j, limit in zip(places, limits) for n, t in enumerate(turns)]

        def both(h, _):
            for at, events in amid.items():
                @pl.when((i == at) & (h == 1))
                def _():
                    for part, level in events:
                        part(level)

            low = 2 * (h * 4 + me.y)
            seen = [span <= low for span in spans]
            alike = [seen[n] | (spans[n] > low + 1) for n in range(2)]
            together = (seen[0] | seen[1]) & alike[0] & alike[1] & jnp.logical_not(last)
            plain = (half == 0) & seen[0] & seen[1]

            @pl.when(together & plain)
            def _():
                attend_item((h, 2 + h), segments_for(low), me.x, False, q2_ref, kv, m_ref, acc_ref)

            @pl.when(together & jnp.logical_not(plain))
            def _():
                attend_item((h, 2 + h), segments_for(low), me.x, True, q2_ref, kv, m_ref, acc_ref)

            @pl.when(jnp.logical_not(together))
            def _():
                lax.fori_loop(0, jnp.where(last, 1, 2), functools.partial(one, h), 0)

            @pl.when((h == 0) & (i == jnp.where(me.z < 4, 5, 7)))
            def _():
                give(0)

            return 0

        def one(h, k, _):
            own = 2 * (h * 4 + me.y) + jnp.where(k == 0, 1 - me.core, me.core)

            @pl.when((spans[0] <= own) | (spans[1] <= own))
            def _():
                attend_item((2 * k + h,), segments_for(own), me.x, True, q2_ref, kv, m_ref, acc_ref)

            return 0

        lax.fori_loop(0, 2, both, 0)

        @pl.when(last)
        def _():
            give(1)
            lax.fori_loop(0, 2, lambda h, _: one(h, 1, 0), 0)

        return 0

    lax.fori_loop(0, 8, step, 0)

    @pl.when(me.z >= 4)
    def _():
        finish(0)

    finish(1)

    arrived(z_kv.at[pl.ds(0, 7)], z_send.at[0])
    arrived(z_q.at[pl.ds(0, 7)], z_send.at[1])
    arrived(kv.at[0, :, pl.ds(0, 3)], x_send.at[0])
    arrived(qall.at[0, :, pl.ds(0, 3)], x_send.at[1])
    for j, ref in enumerate((kv.at[0], kv.at[0], kv.at[0, :, pl.ds(0, 2)], kv.at[0, :, pl.ds(0, 2)])):
        arrived(ref, y_send.at[j])
    arrived(qall.at[0], x_send.at[2])
    for h in range(2):
        arrived(part_out.at[h], sib_send.at[h])
    arrived(out_ref, o_recv)
    arrived(out_ref.at[:, pl.ds(0, (PEERS - 1) * HD)], o_send)


def on_device(query_rows, key_rows, value_rows, token_counts):
    any_spec = pl.BlockSpec(memory_space=pl.ANY)
    dma = pltpu.SemaphoreType.DMA
    return pl.pallas_call(
        kernel,
        out_shape=jax.ShapeDtypeStruct((ROWS, PEERS * HD), jnp.bfloat16),
        in_specs=[pl.BlockSpec(memory_space=pltpu.SMEM), any_spec, any_spec, any_spec],
        out_specs=any_spec,
        scratch_shapes=[
            pltpu.VMEM((3, ROWS, PEERS * HD), jnp.bfloat16), pltpu.VMEM((8, 2, ROWS, 4 * HD), jnp.bfloat16),
            pltpu.VMEM((8, ROWS, 4 * HD), jnp.bfloat16), pltpu.VMEM((4, 8, 4, 2, ROWS, HD), jnp.bfloat16),
            pltpu.VMEM((2, 8, 4, ROWS, HD), jnp.bfloat16),
            pltpu.VMEM((4, LEN, 2 * HD), jnp.bfloat16), pltpu.VMEM((4, LEN, HD), jnp.float32),
            pltpu.VMEM((4, LEN, 2 * HD), jnp.float32), pltpu.VMEM((2, LEN, HD), jnp.bfloat16),
            pltpu.VMEM((2, 2, LEN, HD), jnp.float32), pltpu.VMEM((2, 2, LEN, HD), jnp.float32),
            dma((3,)), dma((2,)), dma((5,)), dma((2,)), dma((3,)), dma((5,)), dma, dma((4,)), dma((5,)), dma((5,)),
            dma((5,)), dma((2,)), dma((2,)), dma, dma],
        compiler_params=pltpu.CompilerParams(collective_id=0, has_side_effects=True, vmem_limit_bytes=VMEM_LIMIT),
        name="span_attention",
    )(token_counts, query_rows, key_rows, value_rows)


def solution(mesh):
    rows = P(("span", "seq"), None)
    return jax.shard_map(
        on_device, mesh=mesh, in_specs=(rows, rows, rows, P()), out_specs=rows, check_vma=False)
```

```python
import functools
import math

import jax
import jax.numpy as jnp
from jax import lax
from jax.experimental import pallas as pl
from jax.experimental.pallas import tpu as pltpu
from jax.sharding import PartitionSpec as P

MESH = pl.DeviceIdType.MESH
HD = 128
SPANS = 16
LEN = 768
ROWS = 48
PART = 192
PEERS = 32
NEG = -1e30
LOG2_SCALE = HD ** -0.5 * math.log2(math.e)
VMEM_LIMIT = 56 * 1024 * 1024


class Place:
    def __init__(self):
        self.span = lax.axis_index("span")
        self.seq = lax.axis_index("seq")
        self.core = self.span % 2
        self.y = (self.span // 2) % 4
        self.z = (self.span // 8) * 4 + self.seq // 4
        self.x = self.seq % 4
        self.sign = 1 - 2 * self.core

    def span_of(self, z_hi, y, core):
        return (z_hi * 4 + y) * 2 + core

    def plane(self, t):
        return (self.z + self.sign * ((t + 1) // 2) * (2 * (t % 2) - 1) + 8) % 8

    def turn_of(self, z, sign):
        d = (sign * (z - self.z) + 8) % 8
        return jnp.where(d > 4, 2 * (8 - d), jnp.maximum(2 * d - 1, 0))

    def peers(self):
        places = {}
        xs = [self.x] + [(self.x + self.sign * dx + 4) % 4 for dx in (1, 2, 3)]
        for t in range(8):
            dz = ((t + 1) // 2) * (2 * (t % 2) - 1)
            z = (self.z + self.sign * dz + 8) % 8
            z_hi, z_lo = z // 4, z % 4
            span = self.span_of(z_hi, self.y, self.core)
            for dx in range(4):
                seq = z_lo * 4 + xs[dx]
                places[t, dx] = ((span, seq), z_hi * 16 + seq)
        return places

    def group(self, g):
        z_hi, z_lo = self.z // 4, self.z % 4
        inner = ((z_lo + 1) // 2) % 2
        other = jnp.where(g == 0, 0, jnp.where(g == 1, 1 - inner, jnp.where(g == 2, inner, 1)))
        moved = jnp.where((g == 1) | (g == 2), 1, 0)
        return (z_hi + other) % 2, (z_lo // 2 + moved) % 2

    def up(self):
        return (self.span_of(self.z // 4, (self.y + self.sign + 4) % 4, self.core), self.seq)

    def down(self):
        return (self.span_of(self.z // 4, (self.y - self.sign + 4) % 4, self.core), self.seq)

    def sibling(self):
        return (self.span_of(self.z // 4, self.y, 1 - self.core), self.seq)


def greet(devices):
    barrier = pltpu.get_barrier_semaphore()
    for device in devices:
        pl.semaphore_signal(barrier, inc=1, device_id=device, device_id_type=MESH)
    pl.semaphore_wait(barrier, len(devices))


def remote(src, dst, send_sem, recv_sem, device):
    return pltpu.make_async_remote_copy(
        src_ref=src, dst_ref=dst, send_sem=send_sem, recv_sem=recv_sem,
        device_id=device, device_id_type=MESH)


def arrived(ref, sem):
    pltpu.make_async_copy(ref, ref, sem).wait()


TILE = 256
HALF = LEN // 2


def attend_item(q_indices, segments, x, sign, masked, q2_ref, kv_ref, m_ref, acc_ref):
    k = jnp.concatenate([kv_ref[j, t, :, 0].reshape(PART, HD) for j, t, _ in segments], axis=0)
    k2 = jnp.concatenate([k, k], axis=1)
    v = jnp.concatenate([kv_ref[j, t, :, 1].reshape(PART, HD) for j, t, _ in segments], axis=0)
    v2 = jnp.concatenate([v, jnp.ones_like(v)], axis=1)
    if masked:
        lane = lax.broadcasted_iota(jnp.int32, (1, PART), 1)
        turn = sum(jnp.where(lane >= n * ROWS, 1, 0) for n in (1, 2, 3))
        at_x = x + sign * turn
        at_x = jnp.where(at_x >= 4, at_x - 4, jnp.where(at_x < 0, at_x + 4, at_x))
        row = lane + (at_x - turn) * ROWS
        bias = jnp.concatenate([jnp.where(row < limit, 0.0, NEG) for _, _, limit in segments], axis=1)
    tiles = [(q, pl.ds(i * TILE, TILE)) for q in q_indices for i in range(LEN // TILE)]
    scores, probs, shrinks = {}, {}, {}

    def score(i):
        q, at = tiles[i]
        scores[i] = lax.dot_general(q2_ref[q, at], k2, (((1,), (1,)), ((), ())), preferred_element_type=jnp.float32)

    def soften(i):
        q, at = tiles[i]
        s = scores.pop(i)
        if masked:
            s = s + bias
        m_old = m_ref[q, at]
        m_new = jnp.maximum(m_old, jnp.max(s, axis=1, keepdims=True))
        probs[i] = jnp.exp2(s - jnp.concatenate([m_new] * (LEN // HD), axis=1)).astype(jnp.bfloat16)
        m_ref[q, at] = m_new
        shrinks[i] = jnp.exp2(m_old - m_new)

    def gain(i):
        q, at = tiles[i]
        shrink = shrinks.pop(i)
        acc_ref[q, at] = acc_ref[q, at] * jnp.concatenate([shrink, shrink], axis=1) + jnp.dot(
            probs.pop(i), v2, preferred_element_type=jnp.float32)

    for i in range(len(tiles) + 2):
        if i < len(tiles):
            score(i)
        if 1 <= i < len(tiles) + 1:
            soften(i - 1)
        if 2 <= i:
            gain(i - 2)


def prepare(i, q, q2_ref, m_ref, acc_ref):
    q = q.astype(jnp.float32) * LOG2_SCALE
    high = q.astype(jnp.bfloat16)
    low = (q - high.astype(jnp.float32)).astype(jnp.bfloat16)
    q2_ref[i] = jnp.concatenate([high, low], axis=1)
    m_ref[i] = jnp.full((LEN, HD), NEG, jnp.float32)
    acc_ref[i] = jnp.zeros((LEN, 2 * HD), jnp.float32)


MIRROR = (0, 2, 1, 4, 3, 6, 5, 7)


LEVELS = ((0, 1), (1, 3), (3, 5), (5, 7), (7, 8))


def kernel(counts_ref, q_ref, k_ref, v_ref, out_ref, stage, z_kv, z_q, kv, qall, q2_ref, m_ref, acc_ref, o_ref,
           part_out, part_in, stage_sem, z_send, z_recv, zq_recv, x_send, x_recv, q_recv, y_send, up_recv, down_recv,
           far_recv, sib_send, part_recv, o_send, o_recv):
    me = Place()
    up, down, sibling = me.up(), me.down(), me.sibling()
    peers = me.peers()
    own_head = peers[0, 0][1]
    z_half = me.z // 4
    staged = [pltpu.make_async_copy(ref, stage.at[i], stage_sem.at[i]) for i, ref in enumerate((k_ref, v_ref, q_ref))]
    for copy in staged:
        copy.start()
    across = [(me.span + 1 - 2 * me.core, peers[0, dx][0][1]) for dx in range(4)]
    greet([device for device, _ in list(peers.values())[1:]] + [up, down] + across)

    def cols(head, heads=1):
        return pl.ds(pl.multiple_of(head * HD, HD), heads * HD)

    x_cols = [cols(peers[0, dx][1] - 4 * me.z) for dx in range(4)]

    def send_z_kv(level):
        for t in range(*LEVELS[level]):
            device, head = peers[t, 0]
            there = MIRROR[t]
            remote(stage.at[pl.ds(0, 2), :, cols(head - me.x, 4)], z_kv.at[there], z_send.at[0],
                   z_recv.at[(there + 1) // 2], device).start()

    def send_z_q(level):
        for t in range(*LEVELS[level]):
            device, head = peers[t, 0]
            there = MIRROR[t]
            remote(stage.at[2, :, cols(head - me.x, 4)], z_q.at[there], z_send.at[1],
                   zq_recv.at[0 if there < 5 else 1], device).start()

    def send_x_kv(level):
        t = pl.ds(LEVELS[level][0], LEVELS[level][1] - LEVELS[level][0])
        if level:
            arrived(z_kv.at[t], z_recv.at[level])
        for dx in range(4):
            if level:
                source, place = z_kv.at[t, :, :, x_cols[dx]], kv.at[0, t, (4 - dx) % 4]
            else:
                source, place = stage.at[pl.ds(0, 2), :, cols(peers[0, dx][1])], kv.at[0, 0, (4 - dx) % 4]
            if dx:
                remote(source, place, x_send.at[0], x_recv.at[level], peers[0, dx][0]).start()
            else:
                pltpu.make_async_copy(source, place, x_recv.at[level]).start()

    def send_x_q(part):
        t = (0, pl.ds(1, 4), pl.ds(5, 3))[part]
        if part:
            arrived(z_q.at[t], zq_recv.at[part - 1])
        for dx in range(4):
            source = z_q.at[t, :, x_cols[dx]] if part else stage.at[2, :, cols(peers[0, dx][1])]
            place = qall.at[1, t, (4 - dx) % 4]
            if dx:
                remote(source, place, x_send.at[1], q_recv, peers[0, dx][0]).start()
            else:
                pltpu.make_async_copy(source, place, q_recv).start()
            remote(source, qall.at[0, t, (4 - dx) % 4], x_send.at[2], q_recv, across[dx]).start()

    def own_part(level):
        t = pl.ds(LEVELS[level][0], LEVELS[level][1] - LEVELS[level][0])
        arrived(kv.at[0, t], x_recv.at[level])
        remote(kv.at[0, t], kv.at[1, t], y_send.at[0], up_recv.at[level], up).start()
        remote(kv.at[0, t], kv.at[2, t], y_send.at[1], down_recv.at[level], down).start()

    def near_part(level):
        t = pl.ds(LEVELS[level][0], LEVELS[level][1] - LEVELS[level][0])
        arrived(kv.at[1, t], up_recv.at[level])
        remote(kv.at[1, t, pl.ds(0, 2)], kv.at[3, t, pl.ds(0, 2)], y_send.at[2], far_recv.at[level], up).start()
        arrived(kv.at[2, t], down_recv.at[level])
        remote(kv.at[2, t, pl.ds(2, 2)], kv.at[3, t, pl.ds(2, 2)], y_send.at[3], far_recv.at[level], down).start()

    def far_part(level):
        t = pl.ds(LEVELS[level][0], LEVELS[level][1] - LEVELS[level][0])
        arrived(kv.at[3, t], far_recv.at[level])

    def give(h):
        lane = lax.broadcasted_iota(jnp.int32, (LEN, HD), 1)
        part_out[h, 0] = acc_ref[h, :, :HD]
        part_out[h, 1] = jnp.where(lane < HD // 2, m_ref[h], acc_ref[h, :, HD:])
        remote(part_out.at[h], part_in.at[h], sib_send.at[h], part_recv.at[h], sibling).start()

    to = cols(own_head)

    def finish(h):
        arrived(part_in.at[h], part_recv.at[h])
        mine, theirs = m_ref[2 + h], part_in[h, 1, :, :1]
        top = jnp.maximum(mine, theirs)
        keep, add = jnp.exp2(mine - top), jnp.exp2(theirs - top)
        total = acc_ref[2 + h, :, HD:] * keep + part_in[h, 1, :, HD // 2:HD // 2 + 1] * add
        o_ref[h] = ((acc_ref[2 + h, :, :HD] * keep + part_in[h, 0] * add) / total).astype(jnp.bfloat16)

        for t in range(8):
            @pl.when(peers[t, 0][1] // 16 == h)
            def _():
                first = pl.multiple_of((peers[t, 0][1] % 16) // 4 * PART, 16)
                for s in range(4):
                    piece = o_ref.at[h, pl.ds(first + s * ROWS, ROWS)]
                    if t or s:
                        remote(piece, out_ref.at[:, to], o_send, o_recv, peers[t, s][0]).start()
                    else:
                        pltpu.make_async_copy(piece, out_ref.at[:, to], o_recv).start()

    def prepare_span(k, h):
        q = [qall[k, me.turn_of(4 * h + z_lo, me.sign * (2 * k - 1))].reshape(PART, HD) for z_lo in range(4)]
        prepare(2 * k + h, jnp.concatenate(q, axis=0), q2_ref, m_ref, acc_ref)

    for copy in staged[:2]:
        copy.wait()
    send_z_kv(1)
    send_x_kv(0)
    staged[2].wait()
    for level in (1, 2, 3, 4):
        send_z_q(level)
    for level in (2, 3, 4):
        send_z_kv(level)
    send_x_q(0)
    own_part(0)
    send_x_kv(1)
    near_part(0)
    own_part(1)
    send_x_q(1)
    near_part(1)
    send_x_q(2)
    far_part(0)
    send_x_kv(2)
    far_part(1)
    arrived(qall, q_recv)
    lax.fori_loop(0, 4, lambda i, _: (prepare_span(i // 2, i % 2), 0)[1], 0)

    before = {1: [(send_x_kv, 3)], 2: [(near_part, 2)], 3: [(far_part, 2), (send_x_kv, 4)], 4: [(near_part, 3)],
              5: [(far_part, 3)], 6: [(near_part, 4)], 7: [(far_part, 4)]}
    amid = {0: [(own_part, 2)], 2: [(own_part, 3)], 4: [(own_part, 4)]}

    def step(i, _):
        g, second = i // 2, i % 2
        for at, events in before.items():
            @pl.when(i == at)
            def _():
                for part, level in events:
                    part(level)

        @pl.when((i == 7) & (me.z < 4))
        def _():
            finish(0)

        z_hi, half = me.group(g)
        plane = z_hi * 4 + half * 2
        turns = (me.turn_of(plane, me.sign), me.turn_of(plane + 1, me.sign))
        places = (jnp.where(second == 0, 1, 0), jnp.where(second == 0, 2, 3))
        ys = [(me.y + jnp.where(second == 0, n * me.sign, f) + 4) % 4 for n, f in ((-1, 0), (1, 2))]

        spans = [2 * (z_hi * 4 + y) + me.core for y in ys]
        last = i == 7

        def segments_for(own):
            limits = [jnp.where(span <= own, counts_ref[span], 0) for span in spans]
            return [(j, t, limit - (half * 2 + n) * PART) for j, limit in zip(places, limits) for n, t in enumerate(turns)]

        def both(h, _):
            for at, events in amid.items():
                @pl.when((i == at) & (h == 1))
                def _():
                    for part, level in events:
                        part(level)

            low = 2 * (h * 4 + me.y)
            seen = [span <= low for span in spans]
            alike = [seen[n] | (spans[n] > low + 1) for n in range(2)]
            together = (seen[0] | seen[1]) & alike[0] & alike[1] & jnp.logical_not(last)
            plain = (half == 0) & seen[0] & seen[1]

            @pl.when(together & plain)
            def _():
                attend_item((h, 2 + h), segments_for(low), me.x, me.sign, False, q2_ref, kv, m_ref, acc_ref)

            @pl.when(together & jnp.logical_not(plain))
            def _():
                attend_item((h, 2 + h), segments_for(low), me.x, me.sign, True, q2_ref, kv, m_ref, acc_ref)

            @pl.when(jnp.logical_not(together))
            def _():
                lax.fori_loop(0, jnp.where(last, 1, 2), functools.partial(one, h), 0)

            @pl.when((h == 0) & (i == jnp.where(me.z < 4, 5, 7)))
            def _():
                give(0)

            return 0

        def one(h, k, _):
            own = 2 * (h * 4 + me.y) + jnp.where(k == 0, 1 - me.core, me.core)

            @pl.when((spans[0] <= own) | (spans[1] <= own))
            def _():
                attend_item((2 * k + h,), segments_for(own), me.x, me.sign, True, q2_ref, kv, m_ref, acc_ref)

            return 0

        lax.fori_loop(0, 2, both, 0)

        @pl.when(last)
        def _():
            give(1)
            lax.fori_loop(0, 2, lambda h, _: one(h, 1, 0), 0)

        return 0

    lax.fori_loop(0, 8, step, 0)

    @pl.when(me.z >= 4)
    def _():
        finish(0)

    finish(1)

    arrived(z_kv.at[pl.ds(0, 7)], z_send.at[0])
    arrived(z_q.at[pl.ds(0, 7)], z_send.at[1])
    arrived(kv.at[0, :, pl.ds(0, 3)], x_send.at[0])
    arrived(qall.at[0, :, pl.ds(0, 3)], x_send.at[1])
    for j, ref in enumerate((kv.at[0], kv.at[0], kv.at[0, :, pl.ds(0, 2)], kv.at[0, :, pl.ds(0, 2)])):
        arrived(ref, y_send.at[j])
    arrived(qall.at[0], x_send.at[2])
    for h in range(2):
        arrived(part_out.at[h], sib_send.at[h])
    arrived(out_ref, o_recv)
    arrived(out_ref.at[:, pl.ds(0, (PEERS - 1) * HD)], o_send)


def on_device(query_rows, key_rows, value_rows, token_counts):
    any_spec = pl.BlockSpec(memory_space=pl.ANY)
    dma = pltpu.SemaphoreType.DMA
    return pl.pallas_call(
        kernel,
        out_shape=jax.ShapeDtypeStruct((ROWS, PEERS * HD), jnp.bfloat16),
        in_specs=[pl.BlockSpec(memory_space=pltpu.SMEM), any_spec, any_spec, any_spec],
        out_specs=any_spec,
        scratch_shapes=[
            pltpu.VMEM((3, ROWS, PEERS * HD), jnp.bfloat16), pltpu.VMEM((8, 2, ROWS, 4 * HD), jnp.bfloat16),
            pltpu.VMEM((8, ROWS, 4 * HD), jnp.bfloat16), pltpu.VMEM((4, 8, 4, 2, ROWS, HD), jnp.bfloat16),
            pltpu.VMEM((2, 8, 4, ROWS, HD), jnp.bfloat16),
            pltpu.VMEM((4, LEN, 2 * HD), jnp.bfloat16), pltpu.VMEM((4, LEN, HD), jnp.float32),
            pltpu.VMEM((4, LEN, 2 * HD), jnp.float32), pltpu.VMEM((2, LEN, HD), jnp.bfloat16),
            pltpu.VMEM((2, 2, LEN, HD), jnp.float32), pltpu.VMEM((2, 2, LEN, HD), jnp.float32),
            dma((3,)), dma((2,)), dma((5,)), dma((2,)), dma((3,)), dma((5,)), dma, dma((4,)), dma((5,)), dma((5,)),
            dma((5,)), dma((2,)), dma((2,)), dma, dma],
        compiler_params=pltpu.CompilerParams(collective_id=0, has_side_effects=True, vmem_limit_bytes=VMEM_LIMIT),
        name="span_attention",
    )(token_counts, query_rows, key_rows, value_rows)


def solution(mesh):
    rows = P(("span", "seq"), None)
    return jax.shard_map(
        on_device, mesh=mesh, in_specs=(rows, rows, rows, P()), out_specs=rows, check_vma=False)
```

```python
import functools
import math

import jax
import jax.numpy as jnp
from jax import lax
from jax.experimental import pallas as pl
from jax.experimental.pallas import tpu as pltpu
from jax.sharding import PartitionSpec as P

MESH = pl.DeviceIdType.MESH
HD = 128
SPANS = 16
LEN = 768
ROWS = 48
PART = 192
PEERS = 32
NEG = -1e30
LOG2_SCALE = HD ** -0.5 * math.log2(math.e)
VMEM_LIMIT = 56 * 1024 * 1024


class Place:
    def __init__(self):
        self.span = lax.axis_index("span")
        self.seq = lax.axis_index("seq")
        self.core = self.span % 2
        self.y = (self.span // 2) % 4
        self.z = (self.span // 8) * 4 + self.seq // 4
        self.x = self.seq % 4
        self.sign = 1 - 2 * self.core

    def span_of(self, z_hi, y, core):
        return (z_hi * 4 + y) * 2 + core

    def plane(self, t):
        return (self.z + self.sign * ((t + 1) // 2) * (2 * (t % 2) - 1) + 8) % 8

    def turn_of(self, z, sign):
        d = (sign * (z - self.z) + 8) % 8
        return jnp.where(d > 4, 2 * (8 - d), jnp.maximum(2 * d - 1, 0))

    def peers(self):
        places = {}
        xs = [self.x] + [(self.x + self.sign * dx + 4) % 4 for dx in (1, 2, 3)]
        for t in range(8):
            dz = ((t + 1) // 2) * (2 * (t % 2) - 1)
            z = (self.z + self.sign * dz + 8) % 8
            z_hi, z_lo = z // 4, z % 4
            span = self.span_of(z_hi, self.y, self.core)
            for dx in range(4):
                seq = z_lo * 4 + xs[dx]
                places[t, dx] = ((span, seq), z_hi * 16 + seq)
        return places

    def group(self, g):
        z_hi, z_lo = self.z // 4, self.z % 4
        inner = ((z_lo + 1) // 2) % 2
        other = jnp.where(g == 0, 0, jnp.where(g == 1, 1 - inner, jnp.where(g == 2, inner, 1)))
        moved = jnp.where((g == 1) | (g == 2), 1, 0)
        return (z_hi + other) % 2, (z_lo // 2 + moved) % 2

    def up(self):
        return (self.span_of(self.z // 4, (self.y + self.sign + 4) % 4, self.core), self.seq)

    def down(self):
        return (self.span_of(self.z // 4, (self.y - self.sign + 4) % 4, self.core), self.seq)

    def sibling(self):
        return (self.span_of(self.z // 4, self.y, 1 - self.core), self.seq)


def greet(devices):
    barrier = pltpu.get_barrier_semaphore()
    for device in devices:
        pl.semaphore_signal(barrier, inc=1, device_id=device, device_id_type=MESH)
    pl.semaphore_wait(barrier, len(devices))


def remote(src, dst, send_sem, recv_sem, device):
    return pltpu.make_async_remote_copy(
        src_ref=src, dst_ref=dst, send_sem=send_sem, recv_sem=recv_sem,
        device_id=device, device_id_type=MESH)


def arrived(ref, sem):
    pltpu.make_async_copy(ref, ref, sem).wait()


TILE = 384
HALF = LEN // 2


def attend_item(q_indices, segments, x, sign, masked, q2_ref, kv_ref, m_ref, acc_ref):
    k = jnp.concatenate([kv_ref[j, t, :, 0].reshape(PART, HD) for j, t, _ in segments], axis=0)
    k2 = jnp.concatenate([k, k], axis=1)
    v = jnp.concatenate([kv_ref[j, t, :, 1].reshape(PART, HD) for j, t, _ in segments], axis=0)
    v2 = jnp.concatenate([v, jnp.ones_like(v)], axis=1)
    if masked:
        lane = lax.broadcasted_iota(jnp.int32, (1, PART), 1)
        turn = sum(jnp.where(lane >= n * ROWS, 1, 0) for n in (1, 2, 3))
        at_x = x + sign * turn
        at_x = jnp.where(at_x >= 4, at_x - 4, jnp.where(at_x < 0, at_x + 4, at_x))
        row = lane + (at_x - turn) * ROWS
        bias = jnp.concatenate([jnp.where(row < limit, 0.0, NEG) for _, _, limit in segments], axis=1)
    tiles = [(q, pl.ds(i * TILE, TILE)) for q in q_indices for i in range(LEN // TILE)]
    scores, probs, shrinks = {}, {}, {}

    def score(i):
        q, at = tiles[i]
        scores[i] = lax.dot_general(q2_ref[q, at], k2, (((1,), (1,)), ((), ())), preferred_element_type=jnp.float32)

    def soften(i):
        q, at = tiles[i]
        s = scores.pop(i)
        if masked:
            s = s + bias
        m_old = m_ref[q, at]
        m_new = jnp.maximum(m_old, jnp.max(s, axis=1, keepdims=True))
        probs[i] = jnp.exp2(s - jnp.concatenate([m_new] * (LEN // HD), axis=1)).astype(jnp.bfloat16)
        m_ref[q, at] = m_new
        shrinks[i] = jnp.exp2(m_old - m_new)

    def gain(i):
        q, at = tiles[i]
        shrink = shrinks.pop(i)
        acc_ref[q, at] = acc_ref[q, at] * jnp.concatenate([shrink, shrink], axis=1) + jnp.dot(
            probs.pop(i), v2, preferred_element_type=jnp.float32)

    for i in range(len(tiles) + 2):
        if i < len(tiles):
            score(i)
        if 1 <= i < len(tiles) + 1:
            soften(i - 1)
        if 2 <= i:
            gain(i - 2)


def prepare(i, q, q2_ref, m_ref, acc_ref):
    q = q.astype(jnp.float32) * LOG2_SCALE
    high = q.astype(jnp.bfloat16)
    low = (q - high.astype(jnp.float32)).astype(jnp.bfloat16)
    q2_ref[i] = jnp.concatenate([high, low], axis=1)
    m_ref[i] = jnp.full((LEN, HD), NEG, jnp.float32)
    acc_ref[i] = jnp.zeros((LEN, 2 * HD), jnp.float32)


MIRROR = (0, 2, 1, 4, 3, 6, 5, 7)


LEVELS = ((0, 1), (1, 3), (3, 5), (5, 7), (7, 8))


def kernel(counts_ref, q_ref, k_ref, v_ref, out_ref, stage, z_kv, z_q, kv, qall, q2_ref, m_ref, acc_ref, o_ref,
           part_out, part_in, stage_sem, z_send, z_recv, zq_recv, x_send, x_recv, q_recv, y_send, up_recv, down_recv,
           far_recv, sib_send, part_recv, o_send, o_recv):
    me = Place()
    up, down, sibling = me.up(), me.down(), me.sibling()
    peers = me.peers()
    own_head = peers[0, 0][1]
    z_half = me.z // 4
    staged = [pltpu.make_async_copy(ref, stage.at[i], stage_sem.at[i]) for i, ref in enumerate((k_ref, v_ref, q_ref))]
    for copy in staged:
        copy.start()
    across = [(me.span + 1 - 2 * me.core, peers[0, dx][0][1]) for dx in range(4)]
    greet([device for device, _ in list(peers.values())[1:]] + [up, down] + across)

    def cols(head, heads=1):
        return pl.ds(pl.multiple_of(head * HD, HD), heads * HD)

    x_cols = [cols(peers[0, dx][1] - 4 * me.z) for dx in range(4)]

    def send_z_kv(level):
        for t in range(*LEVELS[level]):
            device, head = peers[t, 0]
            there = MIRROR[t]
            remote(stage.at[pl.ds(0, 2), :, cols(head - me.x, 4)], z_kv.at[there], z_send.at[0],
                   z_recv.at[(there + 1) // 2], device).start()

    def send_z_q(level):
        for t in range(*LEVELS[level]):
            device, head = peers[t, 0]
            there = MIRROR[t]
            remote(stage.at[2, :, cols(head - me.x, 4)], z_q.at[there], z_send.at[1],
                   zq_recv.at[0 if there < 5 else 1], device).start()

    def send_x_kv(level):
        t = pl.ds(LEVELS[level][0], LEVELS[level][1] - LEVELS[level][0])
        if level:
            arrived(z_kv.at[t], z_recv.at[level])
        for dx in range(4):
            if level:
                source, place = z_kv.at[t, :, :, x_cols[dx]], kv.at[0, t, (4 - dx) % 4]
            else:
                source, place = stage.at[pl.ds(0, 2), :, cols(peers[0, dx][1])], kv.at[0, 0, (4 - dx) % 4]
            if dx:
                remote(source, place, x_send.at[0], x_recv.at[level], peers[0, dx][0]).start()
            else:
                pltpu.make_async_copy(source, place, x_recv.at[level]).start()

    def send_x_q(part):
        t = (0, pl.ds(1, 4), pl.ds(5, 3))[part]
        if part:
            arrived(z_q.at[t], zq_recv.at[part - 1])
        for dx in range(4):
            source = z_q.at[t, :, x_cols[dx]] if part else stage.at[2, :, cols(peers[0, dx][1])]
            place = qall.at[1, t, (4 - dx) % 4]
            if dx:
                remote(source, place, x_send.at[1], q_recv, peers[0, dx][0]).start()
            else:
                pltpu.make_async_copy(source, place, q_recv).start()
            remote(source, qall.at[0, t, (4 - dx) % 4], x_send.at[2], q_recv, across[dx]).start()

    def own_part(level):
        t = pl.ds(LEVELS[level][0], LEVELS[level][1] - LEVELS[level][0])
        arrived(kv.at[0, t], x_recv.at[level])
        remote(kv.at[0, t], kv.at[1, t], y_send.at[0], up_recv.at[level], up).start()
        remote(kv.at[0, t], kv.at[2, t], y_send.at[1], down_recv.at[level], down).start()

    def near_part(level):
        t = pl.ds(LEVELS[level][0], LEVELS[level][1] - LEVELS[level][0])
        arrived(kv.at[1, t], up_recv.at[level])
        remote(kv.at[1, t, pl.ds(0, 2)], kv.at[3, t, pl.ds(0, 2)], y_send.at[2], far_recv.at[level], up).start()
        arrived(kv.at[2, t], down_recv.at[level])
        remote(kv.at[2, t, pl.ds(2, 2)], kv.at[3, t, pl.ds(2, 2)], y_send.at[3], far_recv.at[level], down).start()

    def far_part(level):
        t = pl.ds(LEVELS[level][0], LEVELS[level][1] - LEVELS[level][0])
        arrived(kv.at[3, t], far_recv.at[level])

    def give(h):
        lane = lax.broadcasted_iota(jnp.int32, (LEN, HD), 1)
        part_out[h, 0] = acc_ref[h, :, :HD]
        part_out[h, 1] = jnp.where(lane < HD // 2, m_ref[h], acc_ref[h, :, HD:])
        remote(part_out.at[h], part_in.at[h], sib_send.at[h], part_recv.at[h], sibling).start()

    to = cols(own_head)

    def finish(h):
        arrived(part_in.at[h], part_recv.at[h])
        mine, theirs = m_ref[2 + h], part_in[h, 1, :, :1]
        top = jnp.maximum(mine, theirs)
        keep, add = jnp.exp2(mine - top), jnp.exp2(theirs - top)
        total = acc_ref[2 + h, :, HD:] * keep + part_in[h, 1, :, HD // 2:HD // 2 + 1] * add
        o_ref[h] = ((acc_ref[2 + h, :, :HD] * keep + part_in[h, 0] * add) / total).astype(jnp.bfloat16)

        for t in range(8):
            @pl.when(peers[t, 0][1] // 16 == h)
            def _():
                first = pl.multiple_of((peers[t, 0][1] % 16) // 4 * PART, 16)
                for s in range(4):
                    piece = o_ref.at[h, pl.ds(first + s * ROWS, ROWS)]
                    if t or s:
                        remote(piece, out_ref.at[:, to], o_send, o_recv, peers[t, s][0]).start()
                    else:
                        pltpu.make_async_copy(piece, out_ref.at[:, to], o_recv).start()

    def prepare_span(k, h):
        q = [qall[k, me.turn_of(4 * h + z_lo, me.sign * (2 * k - 1))].reshape(PART, HD) for z_lo in range(4)]
        prepare(2 * k + h, jnp.concatenate(q, axis=0), q2_ref, m_ref, acc_ref)

    for copy in staged[:2]:
        copy.wait()
    send_z_kv(1)
    send_x_kv(0)
    staged[2].wait()
    for level in (1, 2, 3, 4):
        send_z_q(level)
    for level in (2, 3, 4):
        send_z_kv(level)
    send_x_q(0)
    own_part(0)
    send_x_kv(1)
    near_part(0)
    own_part(1)
    send_x_q(1)
    near_part(1)
    send_x_q(2)
    far_part(0)
    send_x_kv(2)
    far_part(1)
    arrived(qall, q_recv)
    lax.fori_loop(0, 4, lambda i, _: (prepare_span(i // 2, i % 2), 0)[1], 0)

    before = {1: [(send_x_kv, 3)], 2: [(near_part, 2)], 3: [(far_part, 2), (send_x_kv, 4)], 4: [(near_part, 3)],
              5: [(far_part, 3)], 6: [(near_part, 4)], 7: [(far_part, 4)]}
    amid = {0: [(own_part, 2)], 2: [(own_part, 3)], 4: [(own_part, 4)]}

    def step(i, _):
        g, second = i // 2, i % 2
        for at, events in before.items():
            @pl.when(i == at)
            def _():
                for part, level in events:
                    part(level)

        @pl.when((i == 7) & (me.z < 4))
        def _():
            finish(0)

        z_hi, half = me.group(g)
        plane = z_hi * 4 + half * 2
        turns = (me.turn_of(plane, me.sign), me.turn_of(plane + 1, me.sign))
        places = (jnp.where(second == 0, 1, 0), jnp.where(second == 0, 2, 3))
        ys = [(me.y + jnp.where(second == 0, n * me.sign, f) + 4) % 4 for n, f in ((-1, 0), (1, 2))]

        spans = [2 * (z_hi * 4 + y) + me.core for y in ys]
        last = i == 7

        def segments_for(own):
            limits = [jnp.where(span <= own, counts_ref[span], 0) for span in spans]
            return [(j, t, limit - (half * 2 + n) * PART) for j, limit in zip(places, limits) for n, t in enumerate(turns)]

        def both(h, _):
            for at, events in amid.items():
                @pl.when((i == at) & (h == 1))
                def _():
                    for part, level in events:
                        part(level)

            low = 2 * (h * 4 + me.y)
            seen = [span <= low for span in spans]
            alike = [seen[n] | (spans[n] > low + 1) for n in range(2)]
            together = (seen[0] | seen[1]) & alike[0] & alike[1] & jnp.logical_not(last)
            plain = (half == 0) & seen[0] & seen[1]

            @pl.when(together & plain)
            def _():
                attend_item((h, 2 + h), segments_for(low), me.x, me.sign, False, q2_ref, kv, m_ref, acc_ref)

            @pl.when(together & jnp.logical_not(plain))
            def _():
                attend_item((h, 2 + h), segments_for(low), me.x, me.sign, True, q2_ref, kv, m_ref, acc_ref)

            @pl.when(jnp.logical_not(together))
            def _():
                lax.fori_loop(0, jnp.where(last, 1, 2), functools.partial(one, h), 0)

            @pl.when((h == 0) & (i == jnp.where(me.z < 4, 5, 7)))
            def _():
                give(0)

            return 0

        def one(h, k, _):
            own = 2 * (h * 4 + me.y) + jnp.where(k == 0, 1 - me.core, me.core)

            @pl.when((spans[0] <= own) | (spans[1] <= own))
            def _():
                attend_item((2 * k + h,), segments_for(own), me.x, me.sign, True, q2_ref, kv, m_ref, acc_ref)

            return 0

        lax.fori_loop(0, 2, both, 0)

        @pl.when(last)
        def _():
            give(1)
            lax.fori_loop(0, 2, lambda h, _: one(h, 1, 0), 0)

        return 0

    lax.fori_loop(0, 8, step, 0)

    @pl.when(me.z >= 4)
    def _():
        finish(0)

    finish(1)

    arrived(z_kv.at[pl.ds(0, 7)], z_send.at[0])
    arrived(z_q.at[pl.ds(0, 7)], z_send.at[1])
    arrived(kv.at[0, :, pl.ds(0, 3)], x_send.at[0])
    arrived(qall.at[0, :, pl.ds(0, 3)], x_send.at[1])
    for j, ref in enumerate((kv.at[0], kv.at[0], kv.at[0, :, pl.ds(0, 2)], kv.at[0, :, pl.ds(0, 2)])):
        arrived(ref, y_send.at[j])
    arrived(qall.at[0], x_send.at[2])
    for h in range(2):
        arrived(part_out.at[h], sib_send.at[h])
    arrived(out_ref, o_recv)
    arrived(out_ref.at[:, pl.ds(0, (PEERS - 1) * HD)], o_send)


def on_device(query_rows, key_rows, value_rows, token_counts):
    any_spec = pl.BlockSpec(memory_space=pl.ANY)
    dma = pltpu.SemaphoreType.DMA
    return pl.pallas_call(
        kernel,
        out_shape=jax.ShapeDtypeStruct((ROWS, PEERS * HD), jnp.bfloat16),
        in_specs=[pl.BlockSpec(memory_space=pltpu.SMEM), any_spec, any_spec, any_spec],
        out_specs=any_spec,
        scratch_shapes=[
            pltpu.VMEM((3, ROWS, PEERS * HD), jnp.bfloat16), pltpu.VMEM((8, 2, ROWS, 4 * HD), jnp.bfloat16),
            pltpu.VMEM((8, ROWS, 4 * HD), jnp.bfloat16), pltpu.VMEM((4, 8, 4, 2, ROWS, HD), jnp.bfloat16),
            pltpu.VMEM((2, 8, 4, ROWS, HD), jnp.bfloat16),
            pltpu.VMEM((4, LEN, 2 * HD), jnp.bfloat16), pltpu.VMEM((4, LEN, HD), jnp.float32),
            pltpu.VMEM((4, LEN, 2 * HD), jnp.float32), pltpu.VMEM((2, LEN, HD), jnp.bfloat16),
            pltpu.VMEM((2, 2, LEN, HD), jnp.float32), pltpu.VMEM((2, 2, LEN, HD), jnp.float32),
            dma((3,)), dma((2,)), dma((5,)), dma((2,)), dma((3,)), dma((5,)), dma, dma((4,)), dma((5,)), dma((5,)),
            dma((5,)), dma((2,)), dma((2,)), dma, dma],
        compiler_params=pltpu.CompilerParams(collective_id=0, has_side_effects=True, vmem_limit_bytes=VMEM_LIMIT),
        name="span_attention",
    )(token_counts, query_rows, key_rows, value_rows)


def solution(mesh):
    rows = P(("span", "seq"), None)
    return jax.shard_map(
        on_device, mesh=mesh, in_specs=(rows, rows, rows, P()), out_specs=rows, check_vma=False)
```

```python
import functools
import math

import jax
import jax.numpy as jnp
from jax import lax
from jax.experimental import pallas as pl
from jax.experimental.pallas import tpu as pltpu
from jax.sharding import PartitionSpec as P

MESH = pl.DeviceIdType.MESH
HD = 128
SPANS = 16
LEN = 768
ROWS = 48
PART = 192
PEERS = 32
NEG = -1e30
LOG2_SCALE = HD ** -0.5 * math.log2(math.e)
VMEM_LIMIT = 56 * 1024 * 1024


class Place:
    def __init__(self):
        self.span = lax.axis_index("span")
        self.seq = lax.axis_index("seq")
        self.core = self.span % 2
        self.y = (self.span // 2) % 4
        self.z = (self.span // 8) * 4 + self.seq // 4
        self.x = self.seq % 4

    def span_of(self, z_hi, y, core):
        return (z_hi * 4 + y) * 2 + core

    def plane(self, t):
        return (self.z + ((t + 1) // 2) * (2 * (t % 2) - 1) + 8) % 8

    def peers(self):
        places = {}
        xs = [self.x] + [(self.x + dx) % 4 for dx in (1, 2, 3)]
        for t in range(8):
            dz = ((t + 1) // 2) * (2 * (t % 2) - 1)
            z = (self.z + dz + 8) % 8
            z_hi, z_lo = z // 4, z % 4
            span = self.span_of(z_hi, self.y, self.core)
            for dx in range(4):
                seq = z_lo * 4 + xs[dx]
                places[t, dx] = ((span, seq), z_hi * 16 + seq)
        return places

    def group(self, g):
        z_hi, z_lo = self.z // 4, self.z % 4
        inner = ((z_lo + 1) // 2) % 2
        other = jnp.where(g == 0, 0, jnp.where(g == 1, 1 - inner, jnp.where(g == 2, inner, 1)))
        moved = jnp.where((g == 1) | (g == 2), 1, 0)
        return (z_hi + other) % 2, (z_lo // 2 + moved) % 2

    def up(self):
        return (self.span_of(self.z // 4, (self.y + 1) % 4, self.core), self.seq)

    def down(self):
        return (self.span_of(self.z // 4, (self.y + 3) % 4, self.core), self.seq)

    def sibling(self):
        return (self.span_of(self.z // 4, self.y, 1 - self.core), self.seq)


def greet(devices):
    barrier = pltpu.get_barrier_semaphore()
    for device in devices:
        pl.semaphore_signal(barrier, inc=1, device_id=device, device_id_type=MESH)
    pl.semaphore_wait(barrier, len(devices))


def remote(src, dst, send_sem, recv_sem, device):
    return pltpu.make_async_remote_copy(
        src_ref=src, dst_ref=dst, send_sem=send_sem, recv_sem=recv_sem,
        device_id=device, device_id_type=MESH)


def arrived(ref, sem):
    pltpu.make_async_copy(ref, ref, sem).wait()


TILE = 256
HALF = LEN // 2


def attend_item(q_index, pair, half, keep_second, counts_ref, q2_ref, kv_ref, m_ref, acc_ref):
    rows = pl.ds(pl.multiple_of(half * HALF, 16), HALF)
    first, second = 2 * pair, 2 * pair + 1
    k = jnp.concatenate([kv_ref[0, first, rows], kv_ref[0, second, rows]], axis=0)
    k2 = jnp.concatenate([k, k], axis=1)
    v = jnp.concatenate([kv_ref[1, first, rows], kv_ref[1, second, rows]], axis=0)
    v2 = jnp.concatenate([v, jnp.ones_like(v)], axis=1)
    lane = lax.broadcasted_iota(jnp.int32, (1, HALF), 1) + half * HALF
    bias = jnp.concatenate([
        jnp.where(lane < counts_ref[first], 0.0, NEG),
        jnp.where(lane < counts_ref[second] * keep_second, 0.0, NEG)], axis=1)
    tiles = LEN // TILE
    scores, probs = [None] * tiles, [None] * tiles

    def at(i):
        return pl.ds(i * TILE, TILE)

    def score(i):
        scores[i] = lax.dot_general(
            q2_ref[q_index, at(i)], k2, (((1,), (1,)), ((), ())), preferred_element_type=jnp.float32)

    def soften(i):
        s = scores[i] + bias
        m_old = m_ref[q_index, at(i)]
        m_new = jnp.maximum(m_old, jnp.max(s, axis=1, keepdims=True))
        wide = jnp.concatenate([m_new] * (LEN // HD), axis=1)
        probs[i] = jnp.exp2(s - wide).astype(jnp.bfloat16)
        m_ref[q_index, at(i)] = m_new
        shrink = jnp.exp2(m_old - m_new)
        acc_ref[q_index, at(i)] = acc_ref[q_index, at(i)] * jnp.concatenate([shrink, shrink], axis=1)

    def gain(i):
        acc_ref[q_index, at(i)] += jnp.dot(probs[i], v2, preferred_element_type=jnp.float32)

    for i in range(tiles + 2):
        if i < tiles:
            score(i)
        if 1 <= i < tiles + 1:
            soften(i - 1)
        if 2 <= i:
            gain(i - 2)


def prepare(z_hi, q_ref, q2_ref, m_ref, acc_ref):
    q = q_ref[z_hi].astype(jnp.float32) * LOG2_SCALE
    high = q.astype(jnp.bfloat16)
    low = (q - high.astype(jnp.float32)).astype(jnp.bfloat16)
    q2_ref[z_hi] = jnp.concatenate([high, low], axis=1)
    m_ref[z_hi] = jnp.full((LEN, HD), NEG, jnp.float32)
    acc_ref[z_hi] = jnp.zeros((LEN, 2 * HD), jnp.float32)


MIRROR = (0, 2, 1, 4, 3, 6, 5, 7)


def messages(*planes):
    return [(t, dx) for dx in range(4) for t in planes if (t, dx) != (0, 0)]


def kernel(counts_ref, q_ref, k_ref, v_ref, out_ref, stage_q, stage_kv, qall, kvall, q2_ref, m_ref, acc_ref, o_ref,
           stage_sem, a2a_send, a2a_recv, q_recv, y_send, up_recv, down_recv, far_recv, sib_recv, o_send, o_recv):
    me = Place()
    up, down, sibling = me.up(), me.down(), me.sibling()
    peers = me.peers()
    own_head = peers[0, 0][1]
    staged = [
        pltpu.make_async_copy(k_ref, stage_kv.at[0], stage_sem.at[0]),
        pltpu.make_async_copy(v_ref, stage_kv.at[1], stage_sem.at[1]),
        pltpu.make_async_copy(q_ref, stage_q, stage_sem.at[2]),
    ]
    for copy in staged:
        copy.start()
    order = messages(0) + messages(1, 2) + messages(3, 4) + messages(5, 6) + messages(7)
    greet([peers[at][0] for at in order] + [up, down, sibling])

    def cols(head):
        return pl.ds(pl.multiple_of(head * HD, HD), HD)

    rows = pl.ds(pl.multiple_of(me.seq * ROWS, 16), ROWS)
    kv_rows = kvall.at[:, me.span, rows]
    q_rows = qall.at[me.z // 4, rows]

    def send_kv(places):
        for t, dx in places:
            device, head = peers[t, dx]
            remote(stage_kv.at[:, :, cols(head)], kv_rows, a2a_send.at[0], a2a_recv.at[MIRROR[t]], device).start()

    def send_q(places):
        for t, dx in places:
            device, head = peers[t, dx]
            remote(stage_q.at[:, cols(head)], q_rows, a2a_send.at[1], q_recv, device).start()

    y_up, y_down, y_far = (me.y + 1) % 4, (me.y + 3) % 4, (me.y + 2) % 4

    def block(t, y, core):
        z = me.plane(t)
        part = pl.ds(pl.multiple_of((z % 4) * PART, 16), PART)
        return me.span_of(z // 4, y, core), part

    def own_part(t):
        span, part = block(t, me.y, me.core)
        ref = kvall.at[:, span, part]
        arrived(ref, a2a_recv.at[t])
        remote(ref, ref, y_send.at[0], up_recv.at[t], up).start()
        remote(ref, ref, y_send.at[1], down_recv.at[t], down).start()
        remote(ref, ref, y_send.at[4], sib_recv.at[t], sibling).start()

    def near_part(t):
        span, part = block(t, y_down, me.core)
        ref = kvall.at[:, span, part]
        arrived(ref, up_recv.at[t])
        half = kvall.at[0, span, part]
        remote(half, half, y_send.at[2], far_recv.at[t], up).start()
        remote(ref, ref, y_send.at[4], sib_recv.at[8 + t], sibling).start()
        span, part = block(t, y_up, me.core)
        ref = kvall.at[:, span, part]
        arrived(ref, down_recv.at[t])
        half = kvall.at[1, span, part]
        remote(half, half, y_send.at[3], far_recv.at[t], down).start()
        remote(ref, ref, y_send.at[4], sib_recv.at[16 + t], sibling).start()

    def far_part(t):
        span, part = block(t, y_far, me.core)
        ref = kvall.at[:, span, part]
        arrived(ref, far_recv.at[t])
        remote(ref, ref, y_send.at[4], sib_recv.at[24 + t], sibling).start()

    def from_sibling(j, y, t):
        span, part = block(t, y, 1 - me.core)
        arrived(kvall.at[:, span, part], sib_recv.at[8 * j + t])

    def each(first, last, part):
        lax.fori_loop(first, last, lambda t, _: (part(t), 0)[1], 0)

    to = cols(own_head)

    def finish(h):
        o_ref[h] = (acc_ref[h, :, :HD] / acc_ref[h, :, HD:]).astype(jnp.bfloat16)

        @pl.when(me.z // 4 == h)
        def _():
            piece = o_ref.at[h, rows]
            pltpu.make_async_copy(piece, out_ref.at[:, to], o_recv).start()

        for place in reversed(order):
            device, head = peers[place]

            @pl.when(head // 16 == h)
            def _():
                piece = o_ref.at[h, pl.ds(pl.multiple_of((head % 16) * ROWS, 16), ROWS)]
                remote(piece, out_ref.at[:, to], o_send, o_recv, device).start()

    for copy in staged[:2]:
        copy.wait()
    pltpu.make_async_copy(stage_kv.at[:, :, to], kv_rows, a2a_recv.at[0]).start()
    send_kv(messages(0))
    send_kv(messages(1, 2))
    staged[2].wait()
    pltpu.make_async_copy(stage_q.at[:, to], q_rows, q_recv).start()
    send_q(order[:14:-1])
    own_part(0)
    send_q(order[14::-1])
    own_part(1)
    own_part(2)
    send_kv(messages(3, 4))
    near_part(0)
    send_kv(messages(5, 6))
    send_kv(messages(7))
    near_part(1)
    near_part(2)
    each(0, 3, far_part)
    arrived(qall, q_recv)
    each(0, 2, lambda h: prepare(h, qall, q2_ref, m_ref, acc_ref))
    each(0, 1, functools.partial(from_sibling, 0, me.y))
    each(0, 1, functools.partial(from_sibling, 1, y_down))
    each(0, 1, functools.partial(from_sibling, 2, y_up))
    each(0, 1, functools.partial(from_sibling, 3, y_far))

    def step(i, _):
        g, j = i // 4, i % 4
        near, far = 2 * g + 1, jnp.minimum(2 * g + 3, 8)
        more, most = 2 * g + 3, jnp.where(g < 3, jnp.minimum(2 * g + 5, 8), 2 * g + 3)

        @pl.when(j == 0)
        def _():
            each(near, far, functools.partial(from_sibling, 0, me.y))

        @pl.when(j == 1)
        def _():
            each(more, jnp.minimum(more + 1, most), own_part)
            each(near, far, functools.partial(from_sibling, 1, y_down))

        @pl.when(j == 2)
        def _():
            each(more + 1, most, own_part)

            @pl.when(g >= 1)
            def _():
                each(near, far, far_part)

            each(near, far, functools.partial(from_sibling, 2, y_up))

        @pl.when(j == 3)
        def _():
            each(more, most, near_part)
            each(near, far, functools.partial(from_sibling, 3, y_far))

        y = (me.y + jnp.where(j == 0, 0, jnp.where(j == 1, 3, jnp.where(j == 2, 1, 2)))) % 4
        z_hi, half = me.group(g)
        pair = z_hi * 4 + y

        def item(q_index, _):
            own = q_index * 4 + me.y

            @pl.when(pair <= own)
            def _():
                keep = jnp.where((pair < own) | (me.core == 1), 1, 0)
                attend_item(q_index, pair, half, keep, counts_ref, q2_ref, kvall, m_ref, acc_ref)

            return 0

        lax.fori_loop(0, 2, item, 0)

        @pl.when((i == 11) & (me.z < 4))
        def _():
            finish(0)

        return 0

    lax.fori_loop(0, 16, step, 0)

    @pl.when(me.z >= 4)
    def _():
        finish(0)

    finish(1)

    sent = pl.ds(0, (PEERS - 1) * HD)
    arrived(stage_kv.at[:, :, sent], a2a_send.at[0])
    arrived(stage_q.at[:, sent], a2a_send.at[1])
    for j, ref in enumerate((kvall.at[:, 0:2], kvall.at[:, 0:2], kvall.at[0, 0:2], kvall.at[0, 0:2], kvall.at[:, 0:8])):
        arrived(ref, y_send.at[j])
    arrived(out_ref, o_recv)
    arrived(out_ref.at[:, sent], o_send)


def on_device(query_rows, key_rows, value_rows, token_counts):
    any_spec = pl.BlockSpec(memory_space=pl.ANY)
    dma = pltpu.SemaphoreType.DMA
    return pl.pallas_call(
        kernel,
        out_shape=jax.ShapeDtypeStruct((ROWS, PEERS * HD), jnp.bfloat16),
        in_specs=[pl.BlockSpec(memory_space=pltpu.SMEM), any_spec, any_spec, any_spec],
        out_specs=any_spec,
        scratch_shapes=[
            pltpu.VMEM((ROWS, PEERS * HD), jnp.bfloat16), pltpu.VMEM((2, ROWS, PEERS * HD), jnp.bfloat16),
            pltpu.VMEM((2, LEN, HD), jnp.bfloat16), pltpu.VMEM((2, SPANS, LEN, HD), jnp.bfloat16),
            pltpu.VMEM((2, LEN, 2 * HD), jnp.bfloat16), pltpu.VMEM((2, LEN, HD), jnp.float32),
            pltpu.VMEM((2, LEN, 2 * HD), jnp.float32), pltpu.VMEM((2, LEN, HD), jnp.bfloat16),
            dma((3,)), dma((2,)), dma((8,)), dma, dma((5,)), dma((8,)), dma((8,)), dma((8,)), dma((32,)), dma, dma],
        compiler_params=pltpu.CompilerParams(collective_id=0, has_side_effects=True, vmem_limit_bytes=VMEM_LIMIT),
        name="span_attention",
    )(token_counts, query_rows, key_rows, value_rows)


def solution(mesh):
    rows = P(("span", "seq"), None)
    return jax.shard_map(
        on_device, mesh=mesh, in_specs=(rows, rows, rows, P()), out_specs=rows, check_vma=False)
```

```python
import functools
import math

import jax
import jax.numpy as jnp
from jax import lax
from jax.experimental import pallas as pl
from jax.experimental.pallas import tpu as pltpu
from jax.sharding import PartitionSpec as P

MESH = pl.DeviceIdType.MESH
HD = 128
SPANS = 16
LEN = 768
ROWS = 48
PART = 192
PEERS = 32
NEG = -1e30
LOG2_SCALE = HD ** -0.5 * math.log2(math.e)
VMEM_LIMIT = 56 * 1024 * 1024


class Place:
    def __init__(self):
        self.span = lax.axis_index("span")
        self.seq = lax.axis_index("seq")
        self.core = self.span % 2
        self.y = (self.span // 2) % 4
        self.z = (self.span // 8) * 4 + self.seq // 4
        self.x = self.seq % 4

    def span_of(self, z_hi, y, core):
        return (z_hi * 4 + y) * 2 + core

    def plane(self, t):
        return (self.z + ((t + 1) // 2) * (2 * (t % 2) - 1) + 8) % 8

    def peers(self):
        places = {}
        xs = [self.x] + [(self.x + dx) % 4 for dx in (1, 2, 3)]
        for t in range(8):
            dz = ((t + 1) // 2) * (2 * (t % 2) - 1)
            z = (self.z + dz + 8) % 8
            z_hi, z_lo = z // 4, z % 4
            span = self.span_of(z_hi, self.y, self.core)
            for dx in range(4):
                seq = z_lo * 4 + xs[dx]
                places[t, dx] = ((span, seq), z_hi * 16 + seq)
        return places

    def group(self, g):
        z_hi, z_lo = self.z // 4, self.z % 4
        inner = ((z_lo + 1) // 2) % 2
        other = jnp.where(g == 0, 0, jnp.where(g == 1, 1 - inner, jnp.where(g == 2, inner, 1)))
        moved = jnp.where((g == 1) | (g == 2), 1, 0)
        return (z_hi + other) % 2, (z_lo // 2 + moved) % 2

    def up(self):
        return (self.span_of(self.z // 4, (self.y + 1) % 4, self.core), self.seq)

    def down(self):
        return (self.span_of(self.z // 4, (self.y + 3) % 4, self.core), self.seq)

    def sibling(self):
        return (self.span_of(self.z // 4, self.y, 1 - self.core), self.seq)


def greet(devices):
    barrier = pltpu.get_barrier_semaphore()
    for device in devices:
        pl.semaphore_signal(barrier, inc=1, device_id=device, device_id_type=MESH)
    pl.semaphore_wait(barrier, len(devices))


def remote(src, dst, send_sem, recv_sem, device):
    return pltpu.make_async_remote_copy(
        src_ref=src, dst_ref=dst, send_sem=send_sem, recv_sem=recv_sem,
        device_id=device, device_id_type=MESH)


def arrived(ref, sem):
    pltpu.make_async_copy(ref, ref, sem).wait()


TILE = 256
HALF = LEN // 2


def attend_item(q_index, pair, half, keep_second, counts_ref, q2_ref, kv_ref, m_ref, acc_ref):
    rows = pl.ds(pl.multiple_of(half * HALF, 16), HALF)
    first, second = 2 * pair, 2 * pair + 1
    k = jnp.concatenate([kv_ref[0, first, rows], kv_ref[0, second, rows]], axis=0)
    k2 = jnp.concatenate([k, k], axis=1)
    v = jnp.concatenate([kv_ref[1, first, rows], kv_ref[1, second, rows]], axis=0)
    v2 = jnp.concatenate([v, jnp.ones_like(v)], axis=1)
    lane = lax.broadcasted_iota(jnp.int32, (1, HALF), 1) + half * HALF
    bias = jnp.concatenate([
        jnp.where(lane < counts_ref[first], 0.0, NEG),
        jnp.where(lane < counts_ref[second] * keep_second, 0.0, NEG)], axis=1)
    tiles = LEN // TILE
    scores, probs = [None] * tiles, [None] * tiles

    def at(i):
        return pl.ds(i * TILE, TILE)

    def score(i):
        scores[i] = lax.dot_general(
            q2_ref[q_index, at(i)], k2, (((1,), (1,)), ((), ())), preferred_element_type=jnp.float32)

    def soften(i):
        s = scores[i] + bias
        m_old = m_ref[q_index, at(i)]
        m_new = jnp.maximum(m_old, jnp.max(s, axis=1, keepdims=True))
        wide = jnp.concatenate([m_new] * (LEN // HD), axis=1)
        probs[i] = jnp.exp2(s - wide).astype(jnp.bfloat16)
        m_ref[q_index, at(i)] = m_new
        shrink = jnp.exp2(m_old - m_new)
        acc_ref[q_index, at(i)] = acc_ref[q_index, at(i)] * jnp.concatenate([shrink, shrink], axis=1)

    def gain(i):
        acc_ref[q_index, at(i)] += jnp.dot(probs[i], v2, preferred_element_type=jnp.float32)

    for i in range(tiles + 2):
        if i < tiles:
            score(i)
        if 1 <= i < tiles + 1:
            soften(i - 1)
        if 2 <= i:
            gain(i - 2)


def prepare(z_hi, q_ref, q2_ref, m_ref, acc_ref):
    q = q_ref[z_hi].astype(jnp.float32) * LOG2_SCALE
    high = q.astype(jnp.bfloat16)
    low = (q - high.astype(jnp.float32)).astype(jnp.bfloat16)
    q2_ref[z_hi] = jnp.concatenate([high, low], axis=1)
    m_ref[z_hi] = jnp.full((LEN, HD), NEG, jnp.float32)
    acc_ref[z_hi] = jnp.zeros((LEN, 2 * HD), jnp.float32)


MIRROR = (0, 2, 1, 4, 3, 6, 5, 7)


def messages(*planes):
    return [(t, dx) for dx in range(4) for t in planes if (t, dx) != (0, 0)]


def kernel(counts_ref, q_ref, k_ref, v_ref, out_ref, stage_q, stage_kv, qall, kvall, q2_ref, m_ref, acc_ref, o_ref,
           stage_sem, a2a_send, a2a_recv, q_recv, y_send, up_recv, down_recv, far_recv, sib_recv, o_send, o_recv):
    me = Place()
    up, down, sibling = me.up(), me.down(), me.sibling()
    peers = me.peers()
    own_head = peers[0, 0][1]
    staged = [
        pltpu.make_async_copy(k_ref, stage_kv.at[0], stage_sem.at[0]),
        pltpu.make_async_copy(v_ref, stage_kv.at[1], stage_sem.at[1]),
        pltpu.make_async_copy(q_ref, stage_q, stage_sem.at[2]),
    ]
    for copy in staged:
        copy.start()
    order = messages(0) + messages(1, 2) + messages(3, 4) + messages(5, 6) + messages(7)
    greet([peers[at][0] for at in order] + [up, down, sibling])

    def cols(head):
        return pl.ds(pl.multiple_of(head * HD, HD), HD)

    rows = pl.ds(pl.multiple_of(me.seq * ROWS, 16), ROWS)
    kv_rows = kvall.at[:, me.span, rows]
    q_rows = qall.at[me.z // 4, rows]

    def send_kv(places):
        for t, dx in places:
            device, head = peers[t, dx]
            remote(stage_kv.at[:, :, cols(head)], kv_rows, a2a_send.at[0], a2a_recv.at[MIRROR[t]], device).start()

    def send_q(places):
        for t, dx in places:
            device, head = peers[t, dx]
            remote(stage_q.at[:, cols(head)], q_rows, a2a_send.at[1], q_recv, device).start()

    y_up, y_down, y_far = (me.y + 1) % 4, (me.y + 3) % 4, (me.y + 2) % 4

    def block(t, y, core):
        z = me.plane(t)
        part = pl.ds(pl.multiple_of((z % 4) * PART, 16), PART)
        return me.span_of(z // 4, y, core), part

    def own_part(t):
        span, part = block(t, me.y, me.core)
        ref = kvall.at[:, span, part]
        arrived(ref, a2a_recv.at[t])
        remote(ref, ref, y_send.at[0], up_recv.at[t], up).start()
        remote(ref, ref, y_send.at[1], down_recv.at[t], down).start()
        remote(ref, ref, y_send.at[4], sib_recv.at[t], sibling).start()

    def near_part(t):
        span, part = block(t, y_down, me.core)
        ref = kvall.at[:, span, part]
        arrived(ref, up_recv.at[t])
        half = kvall.at[0, span, part]
        remote(half, half, y_send.at[2], far_recv.at[t], up).start()
        remote(ref, ref, y_send.at[4], sib_recv.at[8 + t], sibling).start()
        span, part = block(t, y_up, me.core)
        ref = kvall.at[:, span, part]
        arrived(ref, down_recv.at[t])
        half = kvall.at[1, span, part]
        remote(half, half, y_send.at[3], far_recv.at[t], down).start()
        remote(ref, ref, y_send.at[4], sib_recv.at[16 + t], sibling).start()

    def far_part(t):
        span, part = block(t, y_far, me.core)
        ref = kvall.at[:, span, part]
        arrived(ref, far_recv.at[t])
        remote(ref, ref, y_send.at[4], sib_recv.at[24 + t], sibling).start()

    def from_sibling(j, y, t):
        span, part = block(t, y, 1 - me.core)
        arrived(kvall.at[:, span, part], sib_recv.at[8 * j + t])

    def each(first, last, part):
        lax.fori_loop(first, last, lambda t, _: (part(t), 0)[1], 0)

    to = cols(own_head)

    def finish(h):
        o_ref[h] = (acc_ref[h, :, :HD] / acc_ref[h, :, HD:]).astype(jnp.bfloat16)
        for z_lo in range(4):
            for dx in range(4):
                seq = z_lo * 4 + (me.x + dx) % 4
                device = (me.span_of(h, me.y, me.core), seq)
                piece = o_ref.at[h, pl.ds(pl.multiple_of(seq * ROWS, 16), ROWS)]
                own = (me.z == 4 * h + z_lo) if dx == 0 else False

                def send():
                    remote(piece, out_ref.at[:, to], o_send, o_recv, device).start()

                if dx:
                    send()
                else:
                    pl.when(own)(lambda: pltpu.make_async_copy(piece, out_ref.at[:, to], o_recv).start())
                    pl.when(jnp.logical_not(own))(send)

    for copy in staged[:2]:
        copy.wait()
    pltpu.make_async_copy(stage_kv.at[:, :, to], kv_rows, a2a_recv.at[0]).start()
    send_kv(messages(0))
    send_kv(messages(1, 2))
    staged[2].wait()
    pltpu.make_async_copy(stage_q.at[:, to], q_rows, q_recv).start()
    send_q(order[:14:-1])
    own_part(0)
    send_q(order[14::-1])
    own_part(1)
    own_part(2)
    send_kv(messages(3, 4))
    near_part(0)
    send_kv(messages(5, 6))
    send_kv(messages(7))
    near_part(1)
    near_part(2)
    each(0, 3, far_part)
    arrived(qall, q_recv)
    each(0, 2, lambda h: prepare(h, qall, q2_ref, m_ref, acc_ref))
    each(0, 1, functools.partial(from_sibling, 0, me.y))
    each(0, 1, functools.partial(from_sibling, 1, y_down))
    each(0, 1, functools.partial(from_sibling, 2, y_up))
    each(0, 1, functools.partial(from_sibling, 3, y_far))

    def step(i, _):
        again = i >= 16
        g, j = jnp.minimum(i // 4, 3), i % 4
        near, far = 2 * g + 1, jnp.minimum(2 * g + 3, 8)
        more, most = 2 * g + 3, jnp.where(g < 3, jnp.minimum(2 * g + 5, 8), 2 * g + 3)

        @pl.when((j == 0) & jnp.logical_not(again))
        def _():
            each(near, far, functools.partial(from_sibling, 0, me.y))

        @pl.when((j == 1) & jnp.logical_not(again))
        def _():
            each(more, jnp.minimum(more + 1, most), own_part)
            each(near, far, functools.partial(from_sibling, 1, y_down))

        @pl.when((j == 2) & jnp.logical_not(again))
        def _():
            each(more + 1, most, own_part)

            @pl.when(g >= 1)
            def _():
                each(near, far, far_part)

            each(near, far, functools.partial(from_sibling, 2, y_up))

        @pl.when((j == 3) & jnp.logical_not(again))
        def _():
            each(more, most, near_part)
            each(near, far, functools.partial(from_sibling, 3, y_far))

        y = (me.y + jnp.where(j == 0, 0, jnp.where(j == 1, 3, jnp.where(j == 2, 1, 2)))) % 4
        z_hi, half = me.group(g)
        pair = z_hi * 4 + y

        def item(q_index, _):
            own = q_index * 4 + me.y

            @pl.when(pair <= own)
            def _():
                keep = jnp.where((pair < own) | (me.core == 1), 1, 0)
                attend_item(q_index, pair, half, keep, counts_ref, q2_ref, kvall, m_ref, acc_ref)

            return 0

        late = me.z >= 4
        first = jnp.where(again, 1, 0)
        last = jnp.where(again, jnp.where(late, 2, 1), jnp.where((g == 3) & late, 1, 2))
        lax.fori_loop(first, last, item, 0)

        @pl.when(i == jnp.where(late, 15, 11))
        def _():
            finish(0)

        return 0

    lax.fori_loop(0, 20, step, 0)
    finish(1)

    sent = pl.ds(0, (PEERS - 1) * HD)
    arrived(stage_kv.at[:, :, sent], a2a_send.at[0])
    arrived(stage_q.at[:, sent], a2a_send.at[1])
    for j, ref in enumerate((kvall.at[:, 0:2], kvall.at[:, 0:2], kvall.at[0, 0:2], kvall.at[0, 0:2], kvall.at[:, 0:8])):
        arrived(ref, y_send.at[j])
    arrived(out_ref, o_recv)
    arrived(out_ref.at[:, sent], o_send)


def on_device(query_rows, key_rows, value_rows, token_counts):
    any_spec = pl.BlockSpec(memory_space=pl.ANY)
    dma = pltpu.SemaphoreType.DMA
    return pl.pallas_call(
        kernel,
        out_shape=jax.ShapeDtypeStruct((ROWS, PEERS * HD), jnp.bfloat16),
        in_specs=[pl.BlockSpec(memory_space=pltpu.SMEM), any_spec, any_spec, any_spec],
        out_specs=any_spec,
        scratch_shapes=[
            pltpu.VMEM((ROWS, PEERS * HD), jnp.bfloat16), pltpu.VMEM((2, ROWS, PEERS * HD), jnp.bfloat16),
            pltpu.VMEM((2, LEN, HD), jnp.bfloat16), pltpu.VMEM((2, SPANS, LEN, HD), jnp.bfloat16),
            pltpu.VMEM((2, LEN, 2 * HD), jnp.bfloat16), pltpu.VMEM((2, LEN, HD), jnp.float32),
            pltpu.VMEM((2, LEN, 2 * HD), jnp.float32), pltpu.VMEM((2, LEN, HD), jnp.bfloat16),
            dma((3,)), dma((2,)), dma((8,)), dma, dma((5,)), dma((8,)), dma((8,)), dma((8,)), dma((32,)), dma, dma],
        compiler_params=pltpu.CompilerParams(collective_id=0, has_side_effects=True, vmem_limit_bytes=VMEM_LIMIT),
        name="span_attention",
    )(token_counts, query_rows, key_rows, value_rows)


def solution(mesh):
    rows = P(("span", "seq"), None)
    return jax.shard_map(
        on_device, mesh=mesh, in_specs=(rows, rows, rows, P()), out_specs=rows, check_vma=False)
```

```python
import functools
import math

import jax
import jax.numpy as jnp
from jax import lax
from jax.experimental import pallas as pl
from jax.experimental.pallas import tpu as pltpu
from jax.sharding import PartitionSpec as P

MESH = pl.DeviceIdType.MESH
HD = 128
SPANS = 16
LEN = 768
ROWS = 48
PART = 192
PEERS = 32
NEG = -1e30
LOG2_SCALE = HD ** -0.5 * math.log2(math.e)
VMEM_LIMIT = 56 * 1024 * 1024


class Place:
    def __init__(self):
        self.span = lax.axis_index("span")
        self.seq = lax.axis_index("seq")
        self.core = self.span % 2
        self.y = (self.span // 2) % 4
        self.z = (self.span // 8) * 4 + self.seq // 4
        self.x = self.seq % 4

    def span_of(self, z_hi, y, core):
        return (z_hi * 4 + y) * 2 + core

    def plane(self, t):
        return (self.z + ((t + 1) // 2) * (2 * (t % 2) - 1) + 8) % 8

    def peers(self):
        places = {}
        xs = [self.x] + [(self.x + dx) % 4 for dx in (1, 2, 3)]
        for t in range(8):
            dz = ((t + 1) // 2) * (2 * (t % 2) - 1)
            z = (self.z + dz + 8) % 8
            z_hi, z_lo = z // 4, z % 4
            span = self.span_of(z_hi, self.y, self.core)
            for dx in range(4):
                seq = z_lo * 4 + xs[dx]
                places[t, dx] = ((span, seq), z_hi * 16 + seq)
        return places

    def group(self, g):
        z_hi, z_lo = self.z // 4, self.z % 4
        inner = ((z_lo + 1) // 2) % 2
        other = jnp.where(g == 0, 0, jnp.where(g == 1, 1 - inner, jnp.where(g == 2, inner, 1)))
        moved = jnp.where((g == 1) | (g == 2), 1, 0)
        return (z_hi + other) % 2, (z_lo // 2 + moved) % 2

    def up(self):
        return (self.span_of(self.z // 4, (self.y + 1) % 4, self.core), self.seq)

    def down(self):
        return (self.span_of(self.z // 4, (self.y + 3) % 4, self.core), self.seq)

    def sibling(self):
        return (self.span_of(self.z // 4, self.y, 1 - self.core), self.seq)


def greet(devices):
    barrier = pltpu.get_barrier_semaphore()
    for device in devices:
        pl.semaphore_signal(barrier, inc=1, device_id=device, device_id_type=MESH)
    pl.semaphore_wait(barrier, len(devices))


def remote(src, dst, send_sem, recv_sem, device):
    return pltpu.make_async_remote_copy(
        src_ref=src, dst_ref=dst, send_sem=send_sem, recv_sem=recv_sem,
        device_id=device, device_id_type=MESH)


def arrived(ref, sem):
    pltpu.make_async_copy(ref, ref, sem).wait()


TILE = 256
HALF = LEN // 2


def attend_item(q_index, pair, half, keep_second, counts_ref, q2_ref, kv_ref, m_ref, acc_ref):
    rows = pl.ds(pl.multiple_of(half * HALF, 16), HALF)
    first, second = 2 * pair, 2 * pair + 1
    k = jnp.concatenate([kv_ref[0, first, rows], kv_ref[0, second, rows]], axis=0)
    k2 = jnp.concatenate([k, k], axis=1)
    v = jnp.concatenate([kv_ref[1, first, rows], kv_ref[1, second, rows]], axis=0)
    v2 = jnp.concatenate([v, jnp.ones_like(v)], axis=1)
    lane = lax.broadcasted_iota(jnp.int32, (1, HALF), 1) + half * HALF
    bias = jnp.concatenate([
        jnp.where(lane < counts_ref[first], 0.0, NEG),
        jnp.where(lane < counts_ref[second] * keep_second, 0.0, NEG)], axis=1)
    tiles = LEN // TILE
    scores, probs = [None] * tiles, [None] * tiles

    def at(i):
        return pl.ds(i * TILE, TILE)

    def score(i):
        scores[i] = lax.dot_general(
            q2_ref[q_index, at(i)], k2, (((1,), (1,)), ((), ())), preferred_element_type=jnp.float32)

    def soften(i):
        s = scores[i] + bias
        m_old = m_ref[q_index, at(i)]
        m_new = jnp.maximum(m_old, jnp.max(s, axis=1, keepdims=True))
        wide = jnp.concatenate([m_new] * (LEN // HD), axis=1)
        probs[i] = jnp.exp2(s - wide).astype(jnp.bfloat16)
        m_ref[q_index, at(i)] = m_new
        shrink = jnp.exp2(m_old - m_new)
        acc_ref[q_index, at(i)] = acc_ref[q_index, at(i)] * jnp.concatenate([shrink, shrink], axis=1)

    def gain(i):
        acc_ref[q_index, at(i)] += jnp.dot(probs[i], v2, preferred_element_type=jnp.float32)

    for i in range(tiles + 2):
        if i < tiles:
            score(i)
        if 1 <= i < tiles + 1:
            soften(i - 1)
        if 2 <= i:
            gain(i - 2)


def prepare(z_hi, q_ref, q2_ref, m_ref, acc_ref):
    q = q_ref[z_hi].astype(jnp.float32) * LOG2_SCALE
    high = q.astype(jnp.bfloat16)
    low = (q - high.astype(jnp.float32)).astype(jnp.bfloat16)
    q2_ref[z_hi] = jnp.concatenate([high, low], axis=1)
    m_ref[z_hi] = jnp.full((LEN, HD), NEG, jnp.float32)
    acc_ref[z_hi] = jnp.zeros((LEN, 2 * HD), jnp.float32)


MIRROR = (0, 2, 1, 4, 3, 6, 5, 7)


def messages(*planes):
    return [(t, dx) for dx in range(4) for t in planes if (t, dx) != (0, 0)]


def kernel(counts_ref, q_ref, k_ref, v_ref, out_ref, stage_q, stage_kv, qall, kvall, q2_ref, m_ref, acc_ref, o_ref,
           stage_sem, a2a_send, a2a_recv, q_recv, y_send, up_recv, down_recv, far_recv, sib_recv, o_send, o_recv):
    me = Place()
    up, down, sibling = me.up(), me.down(), me.sibling()
    peers = me.peers()
    own_head = peers[0, 0][1]
    staged = [
        pltpu.make_async_copy(k_ref, stage_kv.at[0], stage_sem.at[0]),
        pltpu.make_async_copy(v_ref, stage_kv.at[1], stage_sem.at[1]),
        pltpu.make_async_copy(q_ref, stage_q, stage_sem.at[2]),
    ]
    for copy in staged:
        copy.start()
    order = messages(0) + messages(1, 2) + messages(3, 4) + messages(5, 6) + messages(7)
    greet([peers[at][0] for at in order] + [up, down, sibling])

    def cols(head):
        return pl.ds(pl.multiple_of(head * HD, HD), HD)

    rows = pl.ds(pl.multiple_of(me.seq * ROWS, 16), ROWS)
    kv_rows = kvall.at[:, me.span, rows]
    q_rows = qall.at[me.z // 4, rows]

    def send_kv(places):
        for t, dx in places:
            device, head = peers[t, dx]
            remote(stage_kv.at[:, :, cols(head)], kv_rows, a2a_send.at[0], a2a_recv.at[MIRROR[t]], device).start()

    def send_q(places):
        for t, dx in places:
            device, head = peers[t, dx]
            remote(stage_q.at[:, cols(head)], q_rows, a2a_send.at[1], q_recv, device).start()

    y_up, y_down, y_far = (me.y + 1) % 4, (me.y + 3) % 4, (me.y + 2) % 4

    def block(t, y, core):
        z = me.plane(t)
        part = pl.ds(pl.multiple_of((z % 4) * PART, 16), PART)
        return me.span_of(z // 4, y, core), part

    def own_part(t):
        span, part = block(t, me.y, me.core)
        ref = kvall.at[:, span, part]
        arrived(ref, a2a_recv.at[t])
        remote(ref, ref, y_send.at[0], up_recv.at[t], up).start()
        remote(ref, ref, y_send.at[1], down_recv.at[t], down).start()
        remote(ref, ref, y_send.at[4], sib_recv.at[t], sibling).start()

    def near_part(t):
        span, part = block(t, y_down, me.core)
        ref = kvall.at[:, span, part]
        arrived(ref, up_recv.at[t])
        half = kvall.at[0, span, part]
        remote(half, half, y_send.at[2], far_recv.at[t], up).start()
        remote(ref, ref, y_send.at[4], sib_recv.at[8 + t], sibling).start()
        span, part = block(t, y_up, me.core)
        ref = kvall.at[:, span, part]
        arrived(ref, down_recv.at[t])
        half = kvall.at[1, span, part]
        remote(half, half, y_send.at[3], far_recv.at[t], down).start()
        remote(ref, ref, y_send.at[4], sib_recv.at[16 + t], sibling).start()

    def far_part(t):
        span, part = block(t, y_far, me.core)
        ref = kvall.at[:, span, part]
        arrived(ref, far_recv.at[t])
        remote(ref, ref, y_send.at[4], sib_recv.at[24 + t], sibling).start()

    def from_sibling(j, y, t):
        span, part = block(t, y, 1 - me.core)
        arrived(kvall.at[:, span, part], sib_recv.at[8 * j + t])

    def each(first, last, part):
        lax.fori_loop(first, last, lambda t, _: (part(t), 0)[1], 0)

    to = cols(own_head)

    def finish(h):
        o_ref[h] = (acc_ref[h, :, :HD] / acc_ref[h, :, HD:]).astype(jnp.bfloat16)
        for z_lo in range(4):
            for dx in range(4):
                seq = z_lo * 4 + (me.x + dx) % 4
                device = (me.span_of(h, me.y, me.core), seq)
                piece = o_ref.at[h, pl.ds(pl.multiple_of(seq * ROWS, 16), ROWS)]
                own = (me.z == 4 * h + z_lo) if dx == 0 else False

                def send():
                    remote(piece, out_ref.at[:, to], o_send, o_recv, device).start()

                if dx:
                    send()
                else:
                    pl.when(own)(lambda: pltpu.make_async_copy(piece, out_ref.at[:, to], o_recv).start())
                    pl.when(jnp.logical_not(own))(send)

    for copy in staged[:2]:
        copy.wait()
    pltpu.make_async_copy(stage_kv.at[:, :, to], kv_rows, a2a_recv.at[0]).start()
    send_kv(messages(0))
    send_kv(messages(1, 2))
    staged[2].wait()
    pltpu.make_async_copy(stage_q.at[:, to], q_rows, q_recv).start()
    send_q(order[:14:-1])
    own_part(0)
    send_q(order[14::-1])
    own_part(1)
    own_part(2)
    send_kv(messages(3, 4))
    near_part(0)
    send_kv(messages(5, 6))
    send_kv(messages(7))
    near_part(1)
    near_part(2)
    each(0, 3, far_part)
    each(3, 5, own_part)
    arrived(qall, q_recv)
    each(0, 2, lambda h: prepare(h, qall, q2_ref, m_ref, acc_ref))
    each(0, 1, functools.partial(from_sibling, 0, me.y))
    each(0, 1, functools.partial(from_sibling, 1, y_down))
    each(0, 1, functools.partial(from_sibling, 2, y_up))
    each(0, 1, functools.partial(from_sibling, 3, y_far))

    def step(i, _):
        again = i >= 16
        g, j = jnp.minimum(i // 4, 3), i % 4
        near, far = 2 * g + 1, jnp.minimum(2 * g + 3, 8)
        more, most = jnp.minimum(2 * g + 3, 8), jnp.minimum(2 * g + 5, 8)
        next_more, next_most = jnp.minimum(2 * g + 5, 8), jnp.minimum(2 * g + 7, 8)

        @pl.when((j == 0) & jnp.logical_not(again))
        def _():
            @pl.when(g >= 1)
            def _():
                each(near, far, far_part)

            each(near, far, functools.partial(from_sibling, 0, me.y))

        @pl.when((j == 1) & jnp.logical_not(again))
        def _():
            each(more, most, near_part)
            each(near, far, functools.partial(from_sibling, 1, y_down))

        @pl.when((j == 2) & jnp.logical_not(again))
        def _():
            each(near, far, functools.partial(from_sibling, 2, y_up))

        @pl.when((j == 3) & jnp.logical_not(again))
        def _():
            each(next_more, next_most, own_part)
            each(near, far, functools.partial(from_sibling, 3, y_far))

        y = (me.y + jnp.where(j == 0, 0, jnp.where(j == 1, 3, jnp.where(j == 2, 1, 2)))) % 4
        z_hi, half = me.group(g)
        pair = z_hi * 4 + y

        def item(q_index, _):
            own = q_index * 4 + me.y

            @pl.when(pair <= own)
            def _():
                keep = jnp.where((pair < own) | (me.core == 1), 1, 0)
                attend_item(q_index, pair, half, keep, counts_ref, q2_ref, kvall, m_ref, acc_ref)

            return 0

        late = me.z >= 4
        first = jnp.where(again, 1, 0)
        last = jnp.where(again, jnp.where(late, 2, 1), jnp.where((g == 3) & late, 1, 2))
        lax.fori_loop(first, last, item, 0)

        @pl.when(i == jnp.where(late, 15, 11))
        def _():
            finish(0)

        return 0

    lax.fori_loop(0, 20, step, 0)
    finish(1)

    sent = pl.ds(0, (PEERS - 1) * HD)
    arrived(stage_kv.at[:, :, sent], a2a_send.at[0])
    arrived(stage_q.at[:, sent], a2a_send.at[1])
    for j, ref in enumerate((kvall.at[:, 0:2], kvall.at[:, 0:2], kvall.at[0, 0:2], kvall.at[0, 0:2], kvall.at[:, 0:8])):
        arrived(ref, y_send.at[j])
    arrived(out_ref, o_recv)
    arrived(out_ref.at[:, sent], o_send)


def on_device(query_rows, key_rows, value_rows, token_counts):
    any_spec = pl.BlockSpec(memory_space=pl.ANY)
    dma = pltpu.SemaphoreType.DMA
    return pl.pallas_call(
        kernel,
        out_shape=jax.ShapeDtypeStruct((ROWS, PEERS * HD), jnp.bfloat16),
        in_specs=[pl.BlockSpec(memory_space=pltpu.SMEM), any_spec, any_spec, any_spec],
        out_specs=any_spec,
        scratch_shapes=[
            pltpu.VMEM((ROWS, PEERS * HD), jnp.bfloat16), pltpu.VMEM((2, ROWS, PEERS * HD), jnp.bfloat16),
            pltpu.VMEM((2, LEN, HD), jnp.bfloat16), pltpu.VMEM((2, SPANS, LEN, HD), jnp.bfloat16),
            pltpu.VMEM((2, LEN, 2 * HD), jnp.bfloat16), pltpu.VMEM((2, LEN, HD), jnp.float32),
            pltpu.VMEM((2, LEN, 2 * HD), jnp.float32), pltpu.VMEM((2, LEN, HD), jnp.bfloat16),
            dma((3,)), dma((2,)), dma((8,)), dma, dma((5,)), dma((8,)), dma((8,)), dma((8,)), dma((32,)), dma, dma],
        compiler_params=pltpu.CompilerParams(collective_id=0, has_side_effects=True, vmem_limit_bytes=VMEM_LIMIT),
        name="span_attention",
    )(token_counts, query_rows, key_rows, value_rows)


def solution(mesh):
    rows = P(("span", "seq"), None)
    return jax.shard_map(
        on_device, mesh=mesh, in_specs=(rows, rows, rows, P()), out_specs=rows, check_vma=False)
```

```python
import functools
import math

import jax
import jax.numpy as jnp
from jax import lax
from jax.experimental import pallas as pl
from jax.experimental.pallas import tpu as pltpu
from jax.sharding import PartitionSpec as P

MESH = pl.DeviceIdType.MESH
HD = 128
SPANS = 16
LEN = 768
ROWS = 48
PART = 192
PEERS = 32
NEG = -1e30
LOG2_SCALE = HD ** -0.5 * math.log2(math.e)
VMEM_LIMIT = 56 * 1024 * 1024


class Place:
    def __init__(self):
        self.span = lax.axis_index("span")
        self.seq = lax.axis_index("seq")
        self.core = self.span % 2
        self.y = (self.span // 2) % 4
        self.z = (self.span // 8) * 4 + self.seq // 4
        self.x = self.seq % 4

    def span_of(self, z_hi, y, core):
        return (z_hi * 4 + y) * 2 + core

    def plane(self, t):
        return (self.z + ((t + 1) // 2) * (2 * (t % 2) - 1) + 8) % 8

    def peers(self):
        places = {}
        xs = [self.x] + [(self.x + dx) % 4 for dx in (1, 2, 3)]
        for t in range(8):
            dz = ((t + 1) // 2) * (2 * (t % 2) - 1)
            z = (self.z + dz + 8) % 8
            z_hi, z_lo = z // 4, z % 4
            span = self.span_of(z_hi, self.y, self.core)
            for dx in range(4):
                seq = z_lo * 4 + xs[dx]
                places[t, dx] = ((span, seq), z_hi * 16 + seq)
        return places

    def group(self, g):
        z_hi, z_lo = self.z // 4, self.z % 4
        inner = ((z_lo + 1) // 2) % 2
        other = jnp.where(g == 0, 0, jnp.where(g == 1, 1 - inner, jnp.where(g == 2, inner, 1)))
        moved = jnp.where((g == 1) | (g == 2), 1, 0)
        return (z_hi + other) % 2, (z_lo // 2 + moved) % 2

    def up(self):
        return (self.span_of(self.z // 4, (self.y + 1) % 4, self.core), self.seq)

    def down(self):
        return (self.span_of(self.z // 4, (self.y + 3) % 4, self.core), self.seq)

    def sibling(self):
        return (self.span_of(self.z // 4, self.y, 1 - self.core), self.seq)


def greet(devices):
    barrier = pltpu.get_barrier_semaphore()
    for device in devices:
        pl.semaphore_signal(barrier, inc=1, device_id=device, device_id_type=MESH)
    pl.semaphore_wait(barrier, len(devices))


def remote(src, dst, send_sem, recv_sem, device):
    return pltpu.make_async_remote_copy(
        src_ref=src, dst_ref=dst, send_sem=send_sem, recv_sem=recv_sem,
        device_id=device, device_id_type=MESH)


def arrived(ref, sem):
    pltpu.make_async_copy(ref, ref, sem).wait()


TILE = 256
HALF = LEN // 2


def attend_item(q_index, pair, half, keep_second, masked, counts_ref, q2_ref, kv_ref, m_ref, acc_ref):
    rows = pl.ds(pl.multiple_of(half * HALF, 16), HALF)
    first, second = 2 * pair, 2 * pair + 1
    k = jnp.concatenate([kv_ref[0, first, rows], kv_ref[0, second, rows]], axis=0)
    k2 = jnp.concatenate([k, k], axis=1)
    v = jnp.concatenate([kv_ref[1, first, rows], kv_ref[1, second, rows]], axis=0)
    v2 = jnp.concatenate([v, jnp.ones_like(v)], axis=1)
    if masked:
        lane = lax.broadcasted_iota(jnp.int32, (1, HALF), 1) + half * HALF
        bias = jnp.concatenate([
            jnp.where(lane < counts_ref[first], 0.0, NEG),
            jnp.where(lane < counts_ref[second] * keep_second, 0.0, NEG)], axis=1)
    tiles = LEN // TILE
    scores, probs, shrinks = [None] * tiles, [None] * tiles, [None] * tiles

    def at(i):
        return pl.ds(i * TILE, TILE)

    def score(i):
        scores[i] = lax.dot_general(
            q2_ref[q_index, at(i)], k2, (((1,), (1,)), ((), ())), preferred_element_type=jnp.float32)

    def soften(i):
        s = scores[i] + bias if masked else scores[i]
        m_old = m_ref[q_index, at(i)]
        m_new = jnp.maximum(m_old, jnp.max(s, axis=1, keepdims=True))
        wide = jnp.concatenate([m_new] * (LEN // HD), axis=1)
        probs[i] = jnp.exp2(s - wide).astype(jnp.bfloat16)
        m_ref[q_index, at(i)] = m_new
        shrinks[i] = jnp.exp2(m_old - m_new)

    def gain(i):
        shrink = jnp.concatenate([shrinks[i], shrinks[i]], axis=1)
        acc_ref[q_index, at(i)] = acc_ref[q_index, at(i)] * shrink + jnp.dot(
            probs[i], v2, preferred_element_type=jnp.float32)

    for i in range(tiles + 2):
        if i < tiles:
            score(i)
        if 1 <= i < tiles + 1:
            soften(i - 1)
        if 2 <= i:
            gain(i - 2)


def prepare(z_hi, q_ref, q2_ref, m_ref, acc_ref):
    q = q_ref[z_hi].astype(jnp.float32) * LOG2_SCALE
    high = q.astype(jnp.bfloat16)
    low = (q - high.astype(jnp.float32)).astype(jnp.bfloat16)
    q2_ref[z_hi] = jnp.concatenate([high, low], axis=1)
    m_ref[z_hi] = jnp.full((LEN, HD), NEG, jnp.float32)
    acc_ref[z_hi] = jnp.zeros((LEN, 2 * HD), jnp.float32)


MIRROR = (0, 2, 1, 4, 3, 6, 5, 7)


def messages(*planes):
    return [(t, dx) for dx in range(4) for t in planes if (t, dx) != (0, 0)]


def kernel(counts_ref, q_ref, k_ref, v_ref, out_ref, stage_q, stage_kv, qall, kvall, q2_ref, m_ref, acc_ref, o_ref,
           stage_sem, a2a_send, a2a_recv, q_recv, y_send, up_recv, down_recv, far_recv, sib_recv, o_send, o_recv):
    me = Place()
    up, down, sibling = me.up(), me.down(), me.sibling()
    peers = me.peers()
    own_head = peers[0, 0][1]
    staged = [
        pltpu.make_async_copy(k_ref, stage_kv.at[0], stage_sem.at[0]),
        pltpu.make_async_copy(v_ref, stage_kv.at[1], stage_sem.at[1]),
        pltpu.make_async_copy(q_ref, stage_q, stage_sem.at[2]),
    ]
    for copy in staged:
        copy.start()
    order = messages(0) + messages(1, 2) + messages(3, 4) + messages(5, 6) + messages(7)
    greet([peers[at][0] for at in order] + [up, down, sibling])

    def cols(head):
        return pl.ds(pl.multiple_of(head * HD, HD), HD)

    rows = pl.ds(pl.multiple_of(me.seq * ROWS, 16), ROWS)
    kv_rows = kvall.at[:, me.span, rows]
    q_rows = qall.at[me.z // 4, rows]

    def send_kv(places):
        for t, dx in places:
            device, head = peers[t, dx]
            remote(stage_kv.at[:, :, cols(head)], kv_rows, a2a_send.at[0], a2a_recv.at[MIRROR[t]], device).start()

    def send_q(places):
        for t, dx in places:
            device, head = peers[t, dx]
            remote(stage_q.at[:, cols(head)], q_rows, a2a_send.at[1], q_recv, device).start()

    y_up, y_down, y_far = (me.y + 1) % 4, (me.y + 3) % 4, (me.y + 2) % 4

    def block(t, y, core):
        z = me.plane(t)
        part = pl.ds(pl.multiple_of((z % 4) * PART, 16), PART)
        return me.span_of(z // 4, y, core), part

    def own_part(t):
        span, part = block(t, me.y, me.core)
        ref = kvall.at[:, span, part]
        arrived(ref, a2a_recv.at[t])
        remote(ref, ref, y_send.at[0], up_recv.at[t], up).start()
        remote(ref, ref, y_send.at[1], down_recv.at[t], down).start()
        remote(ref, ref, y_send.at[4], sib_recv.at[t], sibling).start()

    def near_part(t):
        span, part = block(t, y_down, me.core)
        ref = kvall.at[:, span, part]
        arrived(ref, up_recv.at[t])
        half = kvall.at[0, span, part]
        remote(half, half, y_send.at[2], far_recv.at[t], up).start()
        remote(ref, ref, y_send.at[4], sib_recv.at[8 + t], sibling).start()
        span, part = block(t, y_up, me.core)
        ref = kvall.at[:, span, part]
        arrived(ref, down_recv.at[t])
        half = kvall.at[1, span, part]
        remote(half, half, y_send.at[3], far_recv.at[t], down).start()
        remote(ref, ref, y_send.at[4], sib_recv.at[16 + t], sibling).start()

    def far_part(t):
        span, part = block(t, y_far, me.core)
        ref = kvall.at[:, span, part]
        arrived(ref, far_recv.at[t])
        remote(ref, ref, y_send.at[4], sib_recv.at[24 + t], sibling).start()

    def from_sibling(j, y, t):
        span, part = block(t, y, 1 - me.core)
        arrived(kvall.at[:, span, part], sib_recv.at[8 * j + t])

    def each(first, last, part):
        lax.fori_loop(first, last, lambda t, _: (part(t), 0)[1], 0)

    to = cols(own_head)

    def finish(h):
        o_ref[h] = (acc_ref[h, :, :HD] / acc_ref[h, :, HD:]).astype(jnp.bfloat16)
        for z_lo in range(4):
            for dx in range(4):
                seq = z_lo * 4 + (me.x + dx) % 4
                device = (me.span_of(h, me.y, me.core), seq)
                piece = o_ref.at[h, pl.ds(pl.multiple_of(seq * ROWS, 16), ROWS)]
                own = (me.z == 4 * h + z_lo) if dx == 0 else False

                def send():
                    remote(piece, out_ref.at[:, to], o_send, o_recv, device).start()

                if dx:
                    send()
                else:
                    pl.when(own)(lambda: pltpu.make_async_copy(piece, out_ref.at[:, to], o_recv).start())
                    pl.when(jnp.logical_not(own))(send)

    for copy in staged[:2]:
        copy.wait()
    pltpu.make_async_copy(stage_kv.at[:, :, to], kv_rows, a2a_recv.at[0]).start()
    send_kv(messages(0))
    send_kv(messages(1, 2))
    staged[2].wait()
    pltpu.make_async_copy(stage_q.at[:, to], q_rows, q_recv).start()
    send_q(order[:14:-1])
    own_part(0)
    send_q(order[14::-1])
    own_part(1)
    own_part(2)
    send_kv(messages(3, 4))
    near_part(0)
    send_kv(messages(5, 6))
    send_kv(messages(7))
    near_part(1)
    near_part(2)
    each(0, 3, far_part)
    each(3, 5, own_part)
    arrived(qall, q_recv)
    each(0, 2, lambda h: prepare(h, qall, q2_ref, m_ref, acc_ref))
    each(0, 1, functools.partial(from_sibling, 0, me.y))
    each(0, 1, functools.partial(from_sibling, 1, y_down))
    each(0, 1, functools.partial(from_sibling, 2, y_up))
    each(0, 1, functools.partial(from_sibling, 3, y_far))

    def step(i, _):
        again = i >= 16
        g, j = jnp.minimum(i // 4, 3), i % 4
        near, far = 2 * g + 1, jnp.minimum(2 * g + 3, 8)
        more, most = jnp.minimum(2 * g + 3, 8), jnp.minimum(2 * g + 5, 8)
        next_more, next_most = jnp.minimum(2 * g + 5, 8), jnp.minimum(2 * g + 7, 8)

        @pl.when((j == 0) & jnp.logical_not(again))
        def _():
            @pl.when(g >= 1)
            def _():
                each(near, far, far_part)

            each(near, far, functools.partial(from_sibling, 0, me.y))

        @pl.when((j == 1) & jnp.logical_not(again))
        def _():
            each(more, most, near_part)
            each(near, far, functools.partial(from_sibling, 1, y_down))

        @pl.when((j == 2) & jnp.logical_not(again))
        def _():
            each(near, far, functools.partial(from_sibling, 2, y_up))

        @pl.when((j == 3) & jnp.logical_not(again))
        def _():
            each(next_more, next_most, own_part)
            each(near, far, functools.partial(from_sibling, 3, y_far))

        y = (me.y + jnp.where(j == 0, 0, jnp.where(j == 1, 3, jnp.where(j == 2, 1, 2)))) % 4
        z_hi, half = me.group(g)
        pair = z_hi * 4 + y

        def item(q_index, _):
            own = q_index * 4 + me.y

            keep = (pair < own) | (me.core == 1)
            plain = keep & (half == 0)

            def work(masked):
                attend_item(q_index, pair, half, jnp.where(keep, 1, 0), masked, counts_ref, q2_ref, kvall, m_ref, acc_ref)

            pl.when((pair <= own) & plain)(lambda: work(False))
            pl.when((pair <= own) & jnp.logical_not(plain))(lambda: work(True))
            return 0

        late = me.z >= 4
        first = jnp.where(again, 1, 0)
        last = jnp.where(again, jnp.where(late, 2, 1), jnp.where((g == 3) & late, 1, 2))
        lax.fori_loop(first, last, item, 0)

        @pl.when(i == jnp.where(late, 15, 11))
        def _():
            finish(0)

        return 0

    lax.fori_loop(0, 20, step, 0)
    finish(1)

    sent = pl.ds(0, (PEERS - 1) * HD)
    arrived(stage_kv.at[:, :, sent], a2a_send.at[0])
    arrived(stage_q.at[:, sent], a2a_send.at[1])
    for j, ref in enumerate((kvall.at[:, 0:2], kvall.at[:, 0:2], kvall.at[0, 0:2], kvall.at[0, 0:2], kvall.at[:, 0:8])):
        arrived(ref, y_send.at[j])
    arrived(out_ref, o_recv)
    arrived(out_ref.at[:, sent], o_send)


def on_device(query_rows, key_rows, value_rows, token_counts):
    any_spec = pl.BlockSpec(memory_space=pl.ANY)
    dma = pltpu.SemaphoreType.DMA
    return pl.pallas_call(
        kernel,
        out_shape=jax.ShapeDtypeStruct((ROWS, PEERS * HD), jnp.bfloat16),
        in_specs=[pl.BlockSpec(memory_space=pltpu.SMEM), any_spec, any_spec, any_spec],
        out_specs=any_spec,
        scratch_shapes=[
            pltpu.VMEM((ROWS, PEERS * HD), jnp.bfloat16), pltpu.VMEM((2, ROWS, PEERS * HD), jnp.bfloat16),
            pltpu.VMEM((2, LEN, HD), jnp.bfloat16), pltpu.VMEM((2, SPANS, LEN, HD), jnp.bfloat16),
            pltpu.VMEM((2, LEN, 2 * HD), jnp.bfloat16), pltpu.VMEM((2, LEN, HD), jnp.float32),
            pltpu.VMEM((2, LEN, 2 * HD), jnp.float32), pltpu.VMEM((2, LEN, HD), jnp.bfloat16),
            dma((3,)), dma((2,)), dma((8,)), dma, dma((5,)), dma((8,)), dma((8,)), dma((8,)), dma((32,)), dma, dma],
        compiler_params=pltpu.CompilerParams(collective_id=0, has_side_effects=True, vmem_limit_bytes=VMEM_LIMIT),
        name="span_attention",
    )(token_counts, query_rows, key_rows, value_rows)


def solution(mesh):
    rows = P(("span", "seq"), None)
    return jax.shard_map(
        on_device, mesh=mesh, in_specs=(rows, rows, rows, P()), out_specs=rows, check_vma=False)
```

```python
import functools
import math

import jax
import jax.numpy as jnp
from jax import lax
from jax.experimental import pallas as pl
from jax.experimental.pallas import tpu as pltpu
from jax.sharding import PartitionSpec as P

MESH = pl.DeviceIdType.MESH
HD = 128
SPANS = 16
LEN = 768
ROWS = 48
PART = 192
PEERS = 32
NEG = -1e30
LOG2_SCALE = HD ** -0.5 * math.log2(math.e)
VMEM_LIMIT = 56 * 1024 * 1024


class Place:
    def __init__(self):
        self.span = lax.axis_index("span")
        self.seq = lax.axis_index("seq")
        self.core = self.span % 2
        self.y = (self.span // 2) % 4
        self.z = (self.span // 8) * 4 + self.seq // 4
        self.x = self.seq % 4

    def span_of(self, z_hi, y, core):
        return (z_hi * 4 + y) * 2 + core

    def plane(self, t):
        return (self.z + ((t + 1) // 2) * (2 * (t % 2) - 1) + 8) % 8

    def peers(self):
        places = {}
        xs = [self.x] + [(self.x + dx) % 4 for dx in (1, 2, 3)]
        for t in range(8):
            dz = ((t + 1) // 2) * (2 * (t % 2) - 1)
            z = (self.z + dz + 8) % 8
            z_hi, z_lo = z // 4, z % 4
            span = self.span_of(z_hi, self.y, self.core)
            for dx in range(4):
                seq = z_lo * 4 + xs[dx]
                places[t, dx] = ((span, seq), z_hi * 16 + seq)
        return places

    def group(self, g):
        z_hi, z_lo = self.z // 4, self.z % 4
        inner = ((z_lo + 1) // 2) % 2
        other = jnp.where(g == 0, 0, jnp.where(g == 1, 1 - inner, jnp.where(g == 2, inner, 1)))
        moved = jnp.where((g == 1) | (g == 2), 1, 0)
        return (z_hi + other) % 2, (z_lo // 2 + moved) % 2

    def up(self):
        return (self.span_of(self.z // 4, (self.y + 1) % 4, self.core), self.seq)

    def down(self):
        return (self.span_of(self.z // 4, (self.y + 3) % 4, self.core), self.seq)

    def sibling(self):
        return (self.span_of(self.z // 4, self.y, 1 - self.core), self.seq)


def greet(devices):
    barrier = pltpu.get_barrier_semaphore()
    for device in devices:
        pl.semaphore_signal(barrier, inc=1, device_id=device, device_id_type=MESH)
    pl.semaphore_wait(barrier, len(devices))


def remote(src, dst, send_sem, recv_sem, device):
    return pltpu.make_async_remote_copy(
        src_ref=src, dst_ref=dst, send_sem=send_sem, recv_sem=recv_sem,
        device_id=device, device_id_type=MESH)


def arrived(ref, sem):
    pltpu.make_async_copy(ref, ref, sem).wait()


TILE = 256
HALF = LEN // 2


def attend_item(q_index, pair, half, keep_second, counts_ref, q2_ref, kv_ref, m_ref, acc_ref):
    rows = pl.ds(pl.multiple_of(half * HALF, 16), HALF)
    first, second = 2 * pair, 2 * pair + 1
    k = jnp.concatenate([kv_ref[0, first, rows], kv_ref[0, second, rows]], axis=0)
    k2 = jnp.concatenate([k, k], axis=1)
    v = jnp.concatenate([kv_ref[1, first, rows], kv_ref[1, second, rows]], axis=0)
    v2 = jnp.concatenate([v, jnp.ones_like(v)], axis=1)
    lane = lax.broadcasted_iota(jnp.int32, (1, HALF), 1) + half * HALF
    bias = jnp.concatenate([
        jnp.where(lane < counts_ref[first], 0.0, NEG),
        jnp.where(lane < counts_ref[second] * keep_second, 0.0, NEG)], axis=1)
    tiles = LEN // TILE
    scores, probs = [None] * tiles, [None] * tiles

    def at(i):
        return pl.ds(i * TILE, TILE)

    def score(i):
        scores[i] = lax.dot_general(
            q2_ref[q_index, at(i)], k2, (((1,), (1,)), ((), ())), preferred_element_type=jnp.float32)

    def soften(i):
        s = scores[i] + bias
        m_old = m_ref[q_index, at(i)]
        m_new = jnp.maximum(m_old, jnp.max(s, axis=1, keepdims=True))
        wide = jnp.concatenate([m_new] * (LEN // HD), axis=1)
        probs[i] = jnp.exp2(s - wide).astype(jnp.bfloat16)
        m_ref[q_index, at(i)] = m_new
        shrink = jnp.exp2(m_old - m_new)
        acc_ref[q_index, at(i)] = acc_ref[q_index, at(i)] * jnp.concatenate([shrink, shrink], axis=1)

    def gain(i):
        acc_ref[q_index, at(i)] += jnp.dot(probs[i], v2, preferred_element_type=jnp.float32)

    for i in range(tiles + 2):
        if i < tiles:
            score(i)
        if 1 <= i < tiles + 1:
            soften(i - 1)
        if 2 <= i:
            gain(i - 2)


def prepare(z_hi, q_ref, q2_ref, m_ref, acc_ref):
    q = q_ref[z_hi].astype(jnp.float32) * LOG2_SCALE
    high = q.astype(jnp.bfloat16)
    low = (q - high.astype(jnp.float32)).astype(jnp.bfloat16)
    q2_ref[z_hi] = jnp.concatenate([high, low], axis=1)
    m_ref[z_hi] = jnp.full((LEN, HD), NEG, jnp.float32)
    acc_ref[z_hi] = jnp.zeros((LEN, 2 * HD), jnp.float32)


MIRROR = (0, 2, 1, 4, 3, 6, 5, 7)


def messages(*planes):
    return [(t, dx) for dx in range(4) for t in planes if (t, dx) != (0, 0)]


def kernel(counts_ref, q_ref, k_ref, v_ref, out_ref, stage_q, stage_kv, qall, kvall, q2_ref, m_ref, acc_ref, o_ref,
           stage_sem, a2a_send, a2a_recv, q_recv, y_send, up_recv, down_recv, far_recv, sib_recv, o_send, o_recv):
    me = Place()
    up, down, sibling = me.up(), me.down(), me.sibling()
    peers = me.peers()
    own_head = peers[0, 0][1]
    staged = [
        pltpu.make_async_copy(k_ref, stage_kv.at[0], stage_sem.at[0]),
        pltpu.make_async_copy(v_ref, stage_kv.at[1], stage_sem.at[1]),
        pltpu.make_async_copy(q_ref, stage_q, stage_sem.at[2]),
    ]
    for copy in staged:
        copy.start()
    order = messages(0) + messages(1, 2) + messages(3, 4) + messages(5, 6) + messages(7)
    greet([peers[at][0] for at in order] + [up, down, sibling])

    def cols(head):
        return pl.ds(pl.multiple_of(head * HD, HD), HD)

    rows = pl.ds(pl.multiple_of(me.seq * ROWS, 16), ROWS)
    kv_rows = kvall.at[:, me.span, rows]
    q_rows = qall.at[me.z // 4, rows]

    def send_kv(places):
        for t, dx in places:
            device, head = peers[t, dx]
            remote(stage_kv.at[:, :, cols(head)], kv_rows, a2a_send.at[0], a2a_recv.at[MIRROR[t]], device).start()

    def send_q(places):
        for t, dx in places:
            device, head = peers[t, dx]
            remote(stage_q.at[:, cols(head)], q_rows, a2a_send.at[1], q_recv, device).start()

    y_up, y_down, y_far = (me.y + 1) % 4, (me.y + 3) % 4, (me.y + 2) % 4

    def block(t, y, core):
        z = me.plane(t)
        part = pl.ds(pl.multiple_of((z % 4) * PART, 16), PART)
        return me.span_of(z // 4, y, core), part

    def own_part(t):
        span, part = block(t, me.y, me.core)
        ref = kvall.at[:, span, part]
        arrived(ref, a2a_recv.at[t])
        remote(ref, ref, y_send.at[0], up_recv.at[t], up).start()
        remote(ref, ref, y_send.at[1], down_recv.at[t], down).start()
        remote(ref, ref, y_send.at[4], sib_recv.at[t], sibling).start()

    def near_part(t):
        span, part = block(t, y_down, me.core)
        ref = kvall.at[:, span, part]
        arrived(ref, up_recv.at[t])
        half = kvall.at[0, span, part]
        remote(half, half, y_send.at[2], far_recv.at[t], up).start()
        remote(ref, ref, y_send.at[4], sib_recv.at[8 + t], sibling).start()
        span, part = block(t, y_up, me.core)
        ref = kvall.at[:, span, part]
        arrived(ref, down_recv.at[t])
        half = kvall.at[1, span, part]
        remote(half, half, y_send.at[3], far_recv.at[t], down).start()
        remote(ref, ref, y_send.at[4], sib_recv.at[16 + t], sibling).start()

    def far_part(t):
        span, part = block(t, y_far, me.core)
        ref = kvall.at[:, span, part]
        arrived(ref, far_recv.at[t])
        remote(ref, ref, y_send.at[4], sib_recv.at[24 + t], sibling).start()

    def from_sibling(j, y, t):
        span, part = block(t, y, 1 - me.core)
        arrived(kvall.at[:, span, part], sib_recv.at[8 * j + t])

    def each(first, last, part):
        lax.fori_loop(first, last, lambda t, _: (part(t), 0)[1], 0)

    to = cols(own_head)

    def finish(h):
        o_ref[h] = (acc_ref[h, :, :HD] / acc_ref[h, :, HD:]).astype(jnp.bfloat16)
        for z_lo in range(4):
            for dx in range(4):
                seq = z_lo * 4 + (me.x + dx) % 4
                device = (me.span_of(h, me.y, me.core), seq)
                piece = o_ref.at[h, pl.ds(pl.multiple_of(seq * ROWS, 16), ROWS)]
                own = (me.z == 4 * h + z_lo) if dx == 0 else False

                def send():
                    remote(piece, out_ref.at[:, to], o_send, o_recv, device).start()

                if dx:
                    send()
                else:
                    pl.when(own)(lambda: pltpu.make_async_copy(piece, out_ref.at[:, to], o_recv).start())
                    pl.when(jnp.logical_not(own))(send)

    for copy in staged[:2]:
        copy.wait()
    pltpu.make_async_copy(stage_kv.at[:, :, to], kv_rows, a2a_recv.at[0]).start()
    send_kv(messages(0))
    send_kv(messages(1, 2))
    staged[2].wait()
    pltpu.make_async_copy(stage_q.at[:, to], q_rows, q_recv).start()
    send_q(order[::-1])
    send_kv(messages(3, 4))
    send_kv(messages(5, 6))
    send_kv(messages(7))
    own_part(0)
    own_part(1)
    own_part(2)
    near_part(0)
    near_part(1)
    near_part(2)
    each(0, 3, far_part)
    each(3, 5, own_part)
    arrived(qall, q_recv)
    each(0, 2, lambda h: prepare(h, qall, q2_ref, m_ref, acc_ref))
    each(0, 1, functools.partial(from_sibling, 0, me.y))
    each(0, 1, functools.partial(from_sibling, 1, y_down))
    each(0, 1, functools.partial(from_sibling, 2, y_up))
    each(0, 1, functools.partial(from_sibling, 3, y_far))

    def step(i, _):
        again = i >= 16
        g, j = jnp.minimum(i // 4, 3), i % 4
        near, far = 2 * g + 1, jnp.minimum(2 * g + 3, 8)
        more, most = jnp.minimum(2 * g + 3, 8), jnp.minimum(2 * g + 5, 8)
        next_more, next_most = jnp.minimum(2 * g + 5, 8), jnp.minimum(2 * g + 7, 8)

        @pl.when((j == 0) & jnp.logical_not(again))
        def _():
            @pl.when(g >= 1)
            def _():
                each(near, far, far_part)

            each(near, far, functools.partial(from_sibling, 0, me.y))

        @pl.when((j == 1) & jnp.logical_not(again))
        def _():
            each(more, most, near_part)
            each(near, far, functools.partial(from_sibling, 1, y_down))

        @pl.when((j == 2) & jnp.logical_not(again))
        def _():
            each(near, far, functools.partial(from_sibling, 2, y_up))

        @pl.when((j == 3) & jnp.logical_not(again))
        def _():
            each(next_more, next_most, own_part)
            each(near, far, functools.partial(from_sibling, 3, y_far))

        y = (me.y + jnp.where(j == 0, 0, jnp.where(j == 1, 3, jnp.where(j == 2, 1, 2)))) % 4
        z_hi, half = me.group(g)
        pair = z_hi * 4 + y

        def item(q_index, _):
            own = q_index * 4 + me.y

            @pl.when(pair <= own)
            def _():
                keep = jnp.where((pair < own) | (me.core == 1), 1, 0)
                attend_item(q_index, pair, half, keep, counts_ref, q2_ref, kvall, m_ref, acc_ref)

            return 0

        late = me.z >= 4
        first = jnp.where(again, 1, 0)
        last = jnp.where(again, jnp.where(late, 2, 1), jnp.where((g == 3) & late, 1, 2))
        lax.fori_loop(first, last, item, 0)

        @pl.when(i == jnp.where(late, 15, 11))
        def _():
            finish(0)

        return 0

    lax.fori_loop(0, 20, step, 0)
    finish(1)

    sent = pl.ds(0, (PEERS - 1) * HD)
    arrived(stage_kv.at[:, :, sent], a2a_send.at[0])
    arrived(stage_q.at[:, sent], a2a_send.at[1])
    for j, ref in enumerate((kvall.at[:, 0:2], kvall.at[:, 0:2], kvall.at[0, 0:2], kvall.at[0, 0:2], kvall.at[:, 0:8])):
        arrived(ref, y_send.at[j])
    arrived(out_ref, o_recv)
    arrived(out_ref.at[:, sent], o_send)


def on_device(query_rows, key_rows, value_rows, token_counts):
    any_spec = pl.BlockSpec(memory_space=pl.ANY)
    dma = pltpu.SemaphoreType.DMA
    return pl.pallas_call(
        kernel,
        out_shape=jax.ShapeDtypeStruct((ROWS, PEERS * HD), jnp.bfloat16),
        in_specs=[pl.BlockSpec(memory_space=pltpu.SMEM), any_spec, any_spec, any_spec],
        out_specs=any_spec,
        scratch_shapes=[
            pltpu.VMEM((ROWS, PEERS * HD), jnp.bfloat16), pltpu.VMEM((2, ROWS, PEERS * HD), jnp.bfloat16),
            pltpu.VMEM((2, LEN, HD), jnp.bfloat16), pltpu.VMEM((2, SPANS, LEN, HD), jnp.bfloat16),
            pltpu.VMEM((2, LEN, 2 * HD), jnp.bfloat16), pltpu.VMEM((2, LEN, HD), jnp.float32),
            pltpu.VMEM((2, LEN, 2 * HD), jnp.float32), pltpu.VMEM((2, LEN, HD), jnp.bfloat16),
            dma((3,)), dma((2,)), dma((8,)), dma, dma((5,)), dma((8,)), dma((8,)), dma((8,)), dma((32,)), dma, dma],
        compiler_params=pltpu.CompilerParams(collective_id=0, has_side_effects=True, vmem_limit_bytes=VMEM_LIMIT),
        name="span_attention",
    )(token_counts, query_rows, key_rows, value_rows)


def solution(mesh):
    rows = P(("span", "seq"), None)
    return jax.shard_map(
        on_device, mesh=mesh, in_specs=(rows, rows, rows, P()), out_specs=rows, check_vma=False)
```

```python
import functools
import math

import jax
import jax.numpy as jnp
from jax import lax
from jax.experimental import pallas as pl
from jax.experimental.pallas import tpu as pltpu
from jax.sharding import PartitionSpec as P

MESH = pl.DeviceIdType.MESH
HD = 128
SPANS = 16
LEN = 768
ROWS = 48
PART = 192
PEERS = 32
NEG = -1e30
LOG2_SCALE = HD ** -0.5 * math.log2(math.e)
VMEM_LIMIT = 56 * 1024 * 1024


class Place:
    def __init__(self):
        self.span = lax.axis_index("span")
        self.seq = lax.axis_index("seq")
        self.core = self.span % 2
        self.y = (self.span // 2) % 4
        self.z = (self.span // 8) * 4 + self.seq // 4
        self.x = self.seq % 4

    def span_of(self, z_hi, y, core):
        return (z_hi * 4 + y) * 2 + core

    def plane(self, t):
        return (self.z + ((t + 1) // 2) * (2 * (t % 2) - 1) + 8) % 8

    def peers(self):
        places = {}
        xs = [self.x] + [(self.x + dx) % 4 for dx in (1, 2, 3)]
        for t in range(8):
            dz = ((t + 1) // 2) * (2 * (t % 2) - 1)
            z = (self.z + dz + 8) % 8
            z_hi, z_lo = z // 4, z % 4
            span = self.span_of(z_hi, self.y, self.core)
            for dx in range(4):
                seq = z_lo * 4 + xs[dx]
                places[t, dx] = ((span, seq), z_hi * 16 + seq)
        return places

    def group(self, g):
        z_hi, z_lo = self.z // 4, self.z % 4
        inner = ((z_lo + 1) // 2) % 2
        other = jnp.where(g == 0, 0, jnp.where(g == 1, 1 - inner, jnp.where(g == 2, inner, 1)))
        moved = jnp.where((g == 1) | (g == 2), 1, 0)
        return (z_hi + other) % 2, (z_lo // 2 + moved) % 2

    def up(self):
        return (self.span_of(self.z // 4, (self.y + 1) % 4, self.core), self.seq)

    def down(self):
        return (self.span_of(self.z // 4, (self.y + 3) % 4, self.core), self.seq)

    def sibling(self):
        return (self.span_of(self.z // 4, self.y, 1 - self.core), self.seq)


def greet(devices):
    barrier = pltpu.get_barrier_semaphore()
    for device in devices:
        pl.semaphore_signal(barrier, inc=1, device_id=device, device_id_type=MESH)
    pl.semaphore_wait(barrier, len(devices))


def remote(src, dst, send_sem, recv_sem, device):
    return pltpu.make_async_remote_copy(
        src_ref=src, dst_ref=dst, send_sem=send_sem, recv_sem=recv_sem,
        device_id=device, device_id_type=MESH)


def arrived(ref, sem):
    pltpu.make_async_copy(ref, ref, sem).wait()


TILE = 256
HALF = LEN // 2


def attend_item(q_index, pair, half, keep_second, counts_ref, q2_ref, kv_ref, m_ref, acc_ref):
    rows = pl.ds(pl.multiple_of(half * HALF, 16), HALF)
    first, second = 2 * pair, 2 * pair + 1
    k = jnp.concatenate([kv_ref[0, first, rows], kv_ref[0, second, rows]], axis=0)
    k2 = jnp.concatenate([k, k], axis=1)
    v = jnp.concatenate([kv_ref[1, first, rows], kv_ref[1, second, rows]], axis=0)
    v2 = jnp.concatenate([v, jnp.ones_like(v)], axis=1)
    lane = lax.broadcasted_iota(jnp.int32, (1, HALF), 1) + half * HALF
    bias = jnp.concatenate([
        jnp.where(lane < counts_ref[first], 0.0, NEG),
        jnp.where(lane < counts_ref[second] * keep_second, 0.0, NEG)], axis=1)
    tiles = LEN // TILE
    scores, probs = [None] * tiles, [None] * tiles

    def at(i):
        return pl.ds(i * TILE, TILE)

    def score(i):
        scores[i] = lax.dot_general(
            q2_ref[q_index, at(i)], k2, (((1,), (1,)), ((), ())), preferred_element_type=jnp.float32)

    def soften(i):
        s = scores[i] + bias
        m_old = m_ref[q_index, at(i)]
        m_new = jnp.maximum(m_old, jnp.max(s, axis=1, keepdims=True))
        wide = jnp.concatenate([m_new] * (LEN // HD), axis=1)
        probs[i] = jnp.exp2(s - wide).astype(jnp.bfloat16)
        m_ref[q_index, at(i)] = m_new
        shrink = jnp.exp2(m_old - m_new)
        acc_ref[q_index, at(i)] = acc_ref[q_index, at(i)] * jnp.concatenate([shrink, shrink], axis=1)

    def gain(i):
        acc_ref[q_index, at(i)] += jnp.dot(probs[i], v2, preferred_element_type=jnp.float32)

    for i in range(tiles + 2):
        if i < tiles:
            score(i)
        if 1 <= i < tiles + 1:
            soften(i - 1)
        if 2 <= i:
            gain(i - 2)


def prepare(z_hi, q_ref, q2_ref, m_ref, acc_ref):
    q = q_ref[z_hi].astype(jnp.float32) * LOG2_SCALE
    high = q.astype(jnp.bfloat16)
    low = (q - high.astype(jnp.float32)).astype(jnp.bfloat16)
    q2_ref[z_hi] = jnp.concatenate([high, low], axis=1)
    m_ref[z_hi] = jnp.full((LEN, HD), NEG, jnp.float32)
    acc_ref[z_hi] = jnp.zeros((LEN, 2 * HD), jnp.float32)


MIRROR = (0, 2, 1, 4, 3, 6, 5, 7)


def messages(*planes):
    return [(t, dx) for dx in range(4) for t in planes if (t, dx) != (0, 0)]


def kernel(counts_ref, q_ref, k_ref, v_ref, out_ref, stage_q, stage_kv, qall, kvall, q2_ref, m_ref, acc_ref, o_ref,
           stage_sem, a2a_send, a2a_recv, q_recv, y_send, up_recv, down_recv, far_recv, sib_recv, o_send, o_recv):
    me = Place()
    up, down, sibling = me.up(), me.down(), me.sibling()
    peers = me.peers()
    own_head = peers[0, 0][1]
    staged = [
        pltpu.make_async_copy(k_ref, stage_kv.at[0], stage_sem.at[0]),
        pltpu.make_async_copy(v_ref, stage_kv.at[1], stage_sem.at[1]),
        pltpu.make_async_copy(q_ref, stage_q, stage_sem.at[2]),
    ]
    for copy in staged:
        copy.start()
    order = messages(0) + messages(1, 2) + messages(3, 4) + messages(5, 6) + messages(7)
    greet([peers[at][0] for at in order] + [up, down, sibling])

    def cols(head):
        return pl.ds(pl.multiple_of(head * HD, HD), HD)

    rows = pl.ds(pl.multiple_of(me.seq * ROWS, 16), ROWS)
    kv_rows = kvall.at[:, me.span, rows]
    q_rows = qall.at[me.z // 4, rows]

    def send_kv(places):
        for t, dx in places:
            device, head = peers[t, dx]
            remote(stage_kv.at[:, :, cols(head)], kv_rows, a2a_send.at[0], a2a_recv.at[MIRROR[t]], device).start()

    def send_q(places):
        for t, dx in places:
            device, head = peers[t, dx]
            remote(stage_q.at[:, cols(head)], q_rows, a2a_send.at[1], q_recv, device).start()

    y_up, y_down, y_far = (me.y + 1) % 4, (me.y + 3) % 4, (me.y + 2) % 4

    def block(t, y, core):
        z = me.plane(t)
        part = pl.ds(pl.multiple_of((z % 4) * PART, 16), PART)
        return me.span_of(z // 4, y, core), part

    def own_part(t):
        span, part = block(t, me.y, me.core)
        ref = kvall.at[:, span, part]
        arrived(ref, a2a_recv.at[t])
        remote(ref, ref, y_send.at[0], up_recv.at[t], up).start()
        remote(ref, ref, y_send.at[1], down_recv.at[t], down).start()
        remote(ref, ref, y_send.at[4], sib_recv.at[t], sibling).start()

    def near_part(t):
        span, part = block(t, y_down, me.core)
        ref = kvall.at[:, span, part]
        arrived(ref, up_recv.at[t])
        half = kvall.at[0, span, part]
        remote(half, half, y_send.at[2], far_recv.at[t], up).start()
        remote(ref, ref, y_send.at[4], sib_recv.at[8 + t], sibling).start()
        span, part = block(t, y_up, me.core)
        ref = kvall.at[:, span, part]
        arrived(ref, down_recv.at[t])
        half = kvall.at[1, span, part]
        remote(half, half, y_send.at[3], far_recv.at[t], down).start()
        remote(ref, ref, y_send.at[4], sib_recv.at[16 + t], sibling).start()

    def far_part(t):
        span, part = block(t, y_far, me.core)
        ref = kvall.at[:, span, part]
        arrived(ref, far_recv.at[t])
        remote(ref, ref, y_send.at[4], sib_recv.at[24 + t], sibling).start()

    def from_sibling(j, y, t):
        span, part = block(t, y, 1 - me.core)
        arrived(kvall.at[:, span, part], sib_recv.at[8 * j + t])

    def each(first, last, part):
        lax.fori_loop(first, last, lambda t, _: (part(t), 0)[1], 0)

    to = cols(own_head)

    def finish(h):
        o_ref[h] = (acc_ref[h, :, :HD] / acc_ref[h, :, HD:]).astype(jnp.bfloat16)
        for z_lo in range(4):
            for dx in range(4):
                seq = z_lo * 4 + (me.x + dx) % 4
                device = (me.span_of(h, me.y, me.core), seq)
                piece = o_ref.at[h, pl.ds(pl.multiple_of(seq * ROWS, 16), ROWS)]
                own = (me.z == 4 * h + z_lo) if dx == 0 else False

                def send():
                    remote(piece, out_ref.at[:, to], o_send, o_recv, device).start()

                if dx:
                    send()
                else:
                    pl.when(own)(lambda: pltpu.make_async_copy(piece, out_ref.at[:, to], o_recv).start())
                    pl.when(jnp.logical_not(own))(send)

    for copy in staged[:2]:
        copy.wait()
    pltpu.make_async_copy(stage_kv.at[:, :, to], kv_rows, a2a_recv.at[0]).start()
    send_kv(messages(0))
    send_kv(messages(1, 2))
    staged[2].wait()
    pltpu.make_async_copy(stage_q.at[:, to], q_rows, q_recv).start()
    send_q(order[::-1])
    send_kv(messages(7))
    send_kv(messages(5, 6))
    send_kv(messages(3, 4))
    own_part(0)
    own_part(1)
    own_part(2)
    near_part(0)
    near_part(1)
    near_part(2)
    each(0, 3, far_part)
    each(3, 5, own_part)
    arrived(qall, q_recv)
    each(0, 2, lambda h: prepare(h, qall, q2_ref, m_ref, acc_ref))
    each(0, 1, functools.partial(from_sibling, 0, me.y))
    each(0, 1, functools.partial(from_sibling, 1, y_down))
    each(0, 1, functools.partial(from_sibling, 2, y_up))
    each(0, 1, functools.partial(from_sibling, 3, y_far))

    def step(i, _):
        again = i >= 16
        g, j = jnp.minimum(i // 4, 3), i % 4
        near, far = 2 * g + 1, jnp.minimum(2 * g + 3, 8)
        more, most = jnp.minimum(2 * g + 3, 8), jnp.minimum(2 * g + 5, 8)
        next_more, next_most = jnp.minimum(2 * g + 5, 8), jnp.minimum(2 * g + 7, 8)

        @pl.when((j == 0) & jnp.logical_not(again))
        def _():
            @pl.when(g >= 1)
            def _():
                each(near, far, far_part)

            each(near, far, functools.partial(from_sibling, 0, me.y))

        @pl.when((j == 1) & jnp.logical_not(again))
        def _():
            each(more, most, near_part)
            each(near, far, functools.partial(from_sibling, 1, y_down))

        @pl.when((j == 2) & jnp.logical_not(again))
        def _():
            each(near, far, functools.partial(from_sibling, 2, y_up))

        @pl.when((j == 3) & jnp.logical_not(again))
        def _():
            each(next_more, next_most, own_part)
            each(near, far, functools.partial(from_sibling, 3, y_far))

        y = (me.y + jnp.where(j == 0, 0, jnp.where(j == 1, 3, jnp.where(j == 2, 1, 2)))) % 4
        z_hi, half = me.group(g)
        pair = z_hi * 4 + y

        def item(q_index, _):
            own = q_index * 4 + me.y

            @pl.when(pair <= own)
            def _():
                keep = jnp.where((pair < own) | (me.core == 1), 1, 0)
                attend_item(q_index, pair, half, keep, counts_ref, q2_ref, kvall, m_ref, acc_ref)

            return 0

        late = me.z >= 4
        first = jnp.where(again, 1, 0)
        last = jnp.where(again, jnp.where(late, 2, 1), jnp.where((g == 3) & late, 1, 2))
        lax.fori_loop(first, last, item, 0)

        @pl.when(i == jnp.where(late, 15, 11))
        def _():
            finish(0)

        return 0

    lax.fori_loop(0, 20, step, 0)
    finish(1)

    sent = pl.ds(0, (PEERS - 1) * HD)
    arrived(stage_kv.at[:, :, sent], a2a_send.at[0])
    arrived(stage_q.at[:, sent], a2a_send.at[1])
    for j, ref in enumerate((kvall.at[:, 0:2], kvall.at[:, 0:2], kvall.at[0, 0:2], kvall.at[0, 0:2], kvall.at[:, 0:8])):
        arrived(ref, y_send.at[j])
    arrived(out_ref, o_recv)
    arrived(out_ref.at[:, sent], o_send)


def on_device(query_rows, key_rows, value_rows, token_counts):
    any_spec = pl.BlockSpec(memory_space=pl.ANY)
    dma = pltpu.SemaphoreType.DMA
    return pl.pallas_call(
        kernel,
        out_shape=jax.ShapeDtypeStruct((ROWS, PEERS * HD), jnp.bfloat16),
        in_specs=[pl.BlockSpec(memory_space=pltpu.SMEM), any_spec, any_spec, any_spec],
        out_specs=any_spec,
        scratch_shapes=[
            pltpu.VMEM((ROWS, PEERS * HD), jnp.bfloat16), pltpu.VMEM((2, ROWS, PEERS * HD), jnp.bfloat16),
            pltpu.VMEM((2, LEN, HD), jnp.bfloat16), pltpu.VMEM((2, SPANS, LEN, HD), jnp.bfloat16),
            pltpu.VMEM((2, LEN, 2 * HD), jnp.bfloat16), pltpu.VMEM((2, LEN, HD), jnp.float32),
            pltpu.VMEM((2, LEN, 2 * HD), jnp.float32), pltpu.VMEM((2, LEN, HD), jnp.bfloat16),
            dma((3,)), dma((2,)), dma((8,)), dma, dma((5,)), dma((8,)), dma((8,)), dma((8,)), dma((32,)), dma, dma],
        compiler_params=pltpu.CompilerParams(collective_id=0, has_side_effects=True, vmem_limit_bytes=VMEM_LIMIT),
        name="span_attention",
    )(token_counts, query_rows, key_rows, value_rows)


def solution(mesh):
    rows = P(("span", "seq"), None)
    return jax.shard_map(
        on_device, mesh=mesh, in_specs=(rows, rows, rows, P()), out_specs=rows, check_vma=False)
```

```python
import functools
import math

import jax
import jax.numpy as jnp
from jax import lax
from jax.experimental import pallas as pl
from jax.experimental.pallas import tpu as pltpu
from jax.sharding import PartitionSpec as P

MESH = pl.DeviceIdType.MESH
HD = 128
SPANS = 16
LEN = 768
ROWS = 48
PART = 192
PEERS = 32
NEG = -1e30
LOG2_SCALE = HD ** -0.5 * math.log2(math.e)
VMEM_LIMIT = 56 * 1024 * 1024


class Place:
    def __init__(self):
        self.span = lax.axis_index("span")
        self.seq = lax.axis_index("seq")
        self.core = self.span % 2
        self.y = (self.span // 2) % 4
        self.z = (self.span // 8) * 4 + self.seq // 4
        self.x = self.seq % 4

    def span_of(self, z_hi, y, core):
        return (z_hi * 4 + y) * 2 + core

    def plane(self, t):
        return (self.z + ((t + 1) // 2) * (2 * (t % 2) - 1) + 8) % 8

    def peers(self):
        places = {}
        xs = [self.x] + [(self.x + dx) % 4 for dx in (1, 2, 3)]
        for t in range(8):
            dz = ((t + 1) // 2) * (2 * (t % 2) - 1)
            z = (self.z + dz + 8) % 8
            z_hi, z_lo = z // 4, z % 4
            span = self.span_of(z_hi, self.y, self.core)
            for dx in range(4):
                seq = z_lo * 4 + xs[dx]
                places[t, dx] = ((span, seq), z_hi * 16 + seq)
        return places

    def group(self, g):
        z_hi, z_lo = self.z // 4, self.z % 4
        inner = ((z_lo + 1) // 2) % 2
        other = jnp.where(g == 0, 0, jnp.where(g == 1, 1 - inner, jnp.where(g == 2, inner, 1)))
        moved = jnp.where((g == 1) | (g == 2), 1, 0)
        return (z_hi + other) % 2, (z_lo // 2 + moved) % 2

    def up(self):
        return (self.span_of(self.z // 4, (self.y + 1) % 4, self.core), self.seq)

    def down(self):
        return (self.span_of(self.z // 4, (self.y + 3) % 4, self.core), self.seq)

    def sibling(self):
        return (self.span_of(self.z // 4, self.y, 1 - self.core), self.seq)


def greet(devices):
    barrier = pltpu.get_barrier_semaphore()
    for device in devices:
        pl.semaphore_signal(barrier, inc=1, device_id=device, device_id_type=MESH)
    pl.semaphore_wait(barrier, len(devices))


def remote(src, dst, send_sem, recv_sem, device):
    return pltpu.make_async_remote_copy(
        src_ref=src, dst_ref=dst, send_sem=send_sem, recv_sem=recv_sem,
        device_id=device, device_id_type=MESH)


def arrived(ref, sem):
    pltpu.make_async_copy(ref, ref, sem).wait()


TILE = 256
HALF = LEN // 2


def attend_item(q_index, pair, half, keep_second, counts_ref, q2_ref, kv_ref, m_ref, acc_ref):
    rows = pl.ds(pl.multiple_of(half * HALF, 16), HALF)
    first, second = 2 * pair, 2 * pair + 1
    k = jnp.concatenate([kv_ref[0, first, rows], kv_ref[0, second, rows]], axis=0)
    k2 = jnp.concatenate([k, k], axis=1)
    v = jnp.concatenate([kv_ref[1, first, rows], kv_ref[1, second, rows]], axis=0)
    v2 = jnp.concatenate([v, jnp.ones_like(v)], axis=1)
    lane = lax.broadcasted_iota(jnp.int32, (1, HALF), 1) + half * HALF
    bias = jnp.concatenate([
        jnp.where(lane < counts_ref[first], 0.0, NEG),
        jnp.where(lane < counts_ref[second] * keep_second, 0.0, NEG)], axis=1)
    tiles = LEN // TILE
    scores, probs = [None] * tiles, [None] * tiles

    def at(i):
        return pl.ds(i * TILE, TILE)

    def score(i):
        scores[i] = lax.dot_general(
            q2_ref[q_index, at(i)], k2, (((1,), (1,)), ((), ())), preferred_element_type=jnp.float32)

    def soften(i):
        s = scores[i] + bias
        m_old = m_ref[q_index, at(i)]
        m_new = jnp.maximum(m_old, jnp.max(s, axis=1, keepdims=True))
        wide = jnp.concatenate([m_new] * (LEN // HD), axis=1)
        probs[i] = jnp.exp2(s - wide).astype(jnp.bfloat16)
        m_ref[q_index, at(i)] = m_new
        shrink = jnp.exp2(m_old - m_new)
        acc_ref[q_index, at(i)] = acc_ref[q_index, at(i)] * jnp.concatenate([shrink, shrink], axis=1)

    def gain(i):
        acc_ref[q_index, at(i)] += jnp.dot(probs[i], v2, preferred_element_type=jnp.float32)

    for i in range(tiles + 2):
        if i < tiles:
            score(i)
        if 1 <= i < tiles + 1:
            soften(i - 1)
        if 2 <= i:
            gain(i - 2)


def prepare(z_hi, q_ref, q2_ref, m_ref, acc_ref):
    q = q_ref[z_hi].astype(jnp.float32) * LOG2_SCALE
    high = q.astype(jnp.bfloat16)
    low = (q - high.astype(jnp.float32)).astype(jnp.bfloat16)
    q2_ref[z_hi] = jnp.concatenate([high, low], axis=1)
    m_ref[z_hi] = jnp.full((LEN, HD), NEG, jnp.float32)
    acc_ref[z_hi] = jnp.zeros((LEN, 2 * HD), jnp.float32)


MIRROR = (0, 2, 1, 4, 3, 6, 5, 7)


def messages(*planes):
    return [(t, dx) for dx in range(4) for t in planes if (t, dx) != (0, 0)]


def kernel(counts_ref, q_ref, k_ref, v_ref, out_ref, stage_q, stage_kv, qall, kvall, q2_ref, m_ref, acc_ref, o_ref,
           stage_sem, a2a_send, a2a_recv, q_recv, y_send, up_recv, down_recv, far_recv, sib_recv, o_send, o_recv):
    me = Place()
    up, down, sibling = me.up(), me.down(), me.sibling()
    peers = me.peers()
    own_head = peers[0, 0][1]
    staged = [
        pltpu.make_async_copy(k_ref, stage_kv.at[0], stage_sem.at[0]),
        pltpu.make_async_copy(v_ref, stage_kv.at[1], stage_sem.at[1]),
        pltpu.make_async_copy(q_ref, stage_q, stage_sem.at[2]),
    ]
    for copy in staged:
        copy.start()
    order = messages(0) + messages(1, 2) + messages(3, 4) + messages(5, 6) + messages(7)
    greet([peers[at][0] for at in order] + [up, down, sibling])

    def cols(head):
        return pl.ds(pl.multiple_of(head * HD, HD), HD)

    rows = pl.ds(pl.multiple_of(me.seq * ROWS, 16), ROWS)
    kv_rows = kvall.at[:, me.span, rows]
    q_rows = qall.at[me.z // 4, rows]

    def send_kv(places):
        for t, dx in places:
            device, head = peers[t, dx]
            remote(stage_kv.at[:, :, cols(head)], kv_rows, a2a_send.at[0], a2a_recv.at[MIRROR[t]], device).start()

    def send_q(places):
        for t, dx in places:
            device, head = peers[t, dx]
            remote(stage_q.at[:, cols(head)], q_rows, a2a_send.at[1], q_recv, device).start()

    y_up, y_down, y_far = (me.y + 1) % 4, (me.y + 3) % 4, (me.y + 2) % 4

    def block(t, y, core):
        z = me.plane(t)
        part = pl.ds(pl.multiple_of((z % 4) * PART, 16), PART)
        return me.span_of(z // 4, y, core), part

    def own_part(t):
        span, part = block(t, me.y, me.core)
        ref = kvall.at[:, span, part]
        arrived(ref, a2a_recv.at[t])
        remote(ref, ref, y_send.at[0], up_recv.at[t], up).start()
        remote(ref, ref, y_send.at[1], down_recv.at[t], down).start()
        remote(ref, ref, y_send.at[4], sib_recv.at[t], sibling).start()

    def near_part(t):
        span, part = block(t, y_down, me.core)
        ref = kvall.at[:, span, part]
        arrived(ref, up_recv.at[t])
        half = kvall.at[0, span, part]
        remote(half, half, y_send.at[2], far_recv.at[t], up).start()
        remote(ref, ref, y_send.at[4], sib_recv.at[8 + t], sibling).start()
        span, part = block(t, y_up, me.core)
        ref = kvall.at[:, span, part]
        arrived(ref, down_recv.at[t])
        half = kvall.at[1, span, part]
        remote(half, half, y_send.at[3], far_recv.at[t], down).start()
        remote(ref, ref, y_send.at[4], sib_recv.at[16 + t], sibling).start()

    def far_part(t):
        span, part = block(t, y_far, me.core)
        ref = kvall.at[:, span, part]
        arrived(ref, far_recv.at[t])
        remote(ref, ref, y_send.at[4], sib_recv.at[24 + t], sibling).start()

    def from_sibling(j, y, t):
        span, part = block(t, y, 1 - me.core)
        arrived(kvall.at[:, span, part], sib_recv.at[8 * j + t])

    def each(first, last, part):
        lax.fori_loop(first, last, lambda t, _: (part(t), 0)[1], 0)

    to = cols(own_head)

    def finish(h):
        o_ref[h] = (acc_ref[h, :, :HD] / acc_ref[h, :, HD:]).astype(jnp.bfloat16)
        for z_lo in range(4):
            for dx in range(4):
                seq = z_lo * 4 + (me.x + dx) % 4
                device = (me.span_of(h, me.y, me.core), seq)
                piece = o_ref.at[h, pl.ds(pl.multiple_of(seq * ROWS, 16), ROWS)]
                own = (me.z == 4 * h + z_lo) if dx == 0 else False

                def send():
                    remote(piece, out_ref.at[:, to], o_send, o_recv, device).start()

                if dx:
                    send()
                else:
                    pl.when(own)(lambda: pltpu.make_async_copy(piece, out_ref.at[:, to], o_recv).start())
                    pl.when(jnp.logical_not(own))(send)

    for copy in staged[:2]:
        copy.wait()
    pltpu.make_async_copy(stage_kv.at[:, :, to], kv_rows, a2a_recv.at[0]).start()
    send_kv(messages(0))
    send_kv(messages(1, 2))
    send_kv(messages(3, 4))
    staged[2].wait()
    pltpu.make_async_copy(stage_q.at[:, to], q_rows, q_recv).start()
    send_q(order[::-1])
    send_kv(messages(5, 6))
    send_kv(messages(7))
    own_part(0)
    own_part(1)
    own_part(2)
    near_part(0)
    near_part(1)
    near_part(2)
    each(0, 3, far_part)
    each(3, 5, own_part)
    arrived(qall, q_recv)
    each(0, 2, lambda h: prepare(h, qall, q2_ref, m_ref, acc_ref))
    each(0, 1, functools.partial(from_sibling, 0, me.y))
    each(0, 1, functools.partial(from_sibling, 1, y_down))
    each(0, 1, functools.partial(from_sibling, 2, y_up))
    each(0, 1, functools.partial(from_sibling, 3, y_far))

    def step(i, _):
        again = i >= 16
        g, j = jnp.minimum(i // 4, 3), i % 4
        near, far = 2 * g + 1, jnp.minimum(2 * g + 3, 8)
        more, most = jnp.minimum(2 * g + 3, 8), jnp.minimum(2 * g + 5, 8)
        next_more, next_most = jnp.minimum(2 * g + 5, 8), jnp.minimum(2 * g + 7, 8)

        @pl.when((j == 0) & jnp.logical_not(again))
        def _():
            @pl.when(g >= 1)
            def _():
                each(near, far, far_part)

            each(near, far, functools.partial(from_sibling, 0, me.y))

        @pl.when((j == 1) & jnp.logical_not(again))
        def _():
            each(more, most, near_part)
            each(near, far, functools.partial(from_sibling, 1, y_down))

        @pl.when((j == 2) & jnp.logical_not(again))
        def _():
            each(near, far, functools.partial(from_sibling, 2, y_up))

        @pl.when((j == 3) & jnp.logical_not(again))
        def _():
            each(next_more, next_most, own_part)
            each(near, far, functools.partial(from_sibling, 3, y_far))

        y = (me.y + jnp.where(j == 0, 0, jnp.where(j == 1, 3, jnp.where(j == 2, 1, 2)))) % 4
        z_hi, half = me.group(g)
        pair = z_hi * 4 + y

        def item(q_index, _):
            own = q_index * 4 + me.y

            @pl.when(pair <= own)
            def _():
                keep = jnp.where((pair < own) | (me.core == 1), 1, 0)
                attend_item(q_index, pair, half, keep, counts_ref, q2_ref, kvall, m_ref, acc_ref)

            return 0

        late = me.z >= 4
        first = jnp.where(again, 1, 0)
        last = jnp.where(again, jnp.where(late, 2, 1), jnp.where((g == 3) & late, 1, 2))
        lax.fori_loop(first, last, item, 0)

        @pl.when(i == jnp.where(late, 15, 11))
        def _():
            finish(0)

        return 0

    lax.fori_loop(0, 20, step, 0)
    finish(1)

    sent = pl.ds(0, (PEERS - 1) * HD)
    arrived(stage_kv.at[:, :, sent], a2a_send.at[0])
    arrived(stage_q.at[:, sent], a2a_send.at[1])
    for j, ref in enumerate((kvall.at[:, 0:2], kvall.at[:, 0:2], kvall.at[0, 0:2], kvall.at[0, 0:2], kvall.at[:, 0:8])):
        arrived(ref, y_send.at[j])
    arrived(out_ref, o_recv)
    arrived(out_ref.at[:, sent], o_send)


def on_device(query_rows, key_rows, value_rows, token_counts):
    any_spec = pl.BlockSpec(memory_space=pl.ANY)
    dma = pltpu.SemaphoreType.DMA
    return pl.pallas_call(
        kernel,
        out_shape=jax.ShapeDtypeStruct((ROWS, PEERS * HD), jnp.bfloat16),
        in_specs=[pl.BlockSpec(memory_space=pltpu.SMEM), any_spec, any_spec, any_spec],
        out_specs=any_spec,
        scratch_shapes=[
            pltpu.VMEM((ROWS, PEERS * HD), jnp.bfloat16), pltpu.VMEM((2, ROWS, PEERS * HD), jnp.bfloat16),
            pltpu.VMEM((2, LEN, HD), jnp.bfloat16), pltpu.VMEM((2, SPANS, LEN, HD), jnp.bfloat16),
            pltpu.VMEM((2, LEN, 2 * HD), jnp.bfloat16), pltpu.VMEM((2, LEN, HD), jnp.float32),
            pltpu.VMEM((2, LEN, 2 * HD), jnp.float32), pltpu.VMEM((2, LEN, HD), jnp.bfloat16),
            dma((3,)), dma((2,)), dma((8,)), dma, dma((5,)), dma((8,)), dma((8,)), dma((8,)), dma((32,)), dma, dma],
        compiler_params=pltpu.CompilerParams(collective_id=0, has_side_effects=True, vmem_limit_bytes=VMEM_LIMIT),
        name="span_attention",
    )(token_counts, query_rows, key_rows, value_rows)


def solution(mesh):
    rows = P(("span", "seq"), None)
    return jax.shard_map(
        on_device, mesh=mesh, in_specs=(rows, rows, rows, P()), out_specs=rows, check_vma=False)
```
